32 devices in a mesh: ctx: 8 (over z, x), exp: 4 (over y, core).
Axes of the slice: x: 2, y: 2, z: 4, core: 2. Of those that a mesh axis runs over, the one named last changes fastest.
Arguments:
- residual: bfloat16 [4096, 2048], P(('ctx', 'exp')), may hold values from -6 to 6
- mixed_qkv: bfloat16 [4096, 4096], P(('ctx', 'exp')), may hold values from -6 to 6
- output_gate: bfloat16 [4096, 2048], P(('ctx', 'exp')), may hold values from -6 to 6
- log_decay: float32 [4096, 16], P(('ctx', 'exp')), may hold values from -0.8 to 0, as said below
- write_strength: float32 [4096, 16], P(('ctx', 'exp')), may hold values from 0 to 1, as said below
- conv_weight: float32 [4, 4096], replicated, may hold values from -3 to 3
- norm_gain: float32 [128], replicated, may hold values from 0.1 to 1.9
- out_weight: bfloat16 [2048, 2048], P(None, 'exp'), may hold values from -0.125 to 0.125
- post_gain: float32 [2048], replicated, may hold values from 0.1 to 1.9
- router_weight: bfloat16 [2048, 64], replicated, may hold values from -0.125 to 0.125
- expert_ids: int32 [4096, 10], P(('ctx', 'exp')), may hold values from 0 to 63, all different within a row; in each aligned block of 128 rows (0 to 127, 128 to 255, ...) at most 24 rows name the same one
- expert_gate: bfloat16 [64, 2048, 512], P(('ctx', 'exp')), may hold values from -0.125 to 0.125
- expert_up: bfloat16 [64, 2048, 512], P(('ctx', 'exp')), may hold values from -0.125 to 0.125
- expert_down: bfloat16 [64, 512, 2048], P(('ctx', 'exp')), may hold values from -0.25 to 0.25
- shared_gate: bfloat16 [2048, 512], replicated, may hold values from -0.125 to 0.125
- shared_up: bfloat16 [2048, 512], replicated, may hold values from -0.125 to 0.125
- shared_down: bfloat16 [512, 2048], replicated, may hold values from -0.25 to 0.25
- shared_switch: bfloat16 [2048], replicated, may hold values from -0.125 to 0.125
Outputs:
- layer_out: bfloat16 [4096, 2048], P(('ctx', 'exp'))
The draws below stay inside these ranges and needn't reach their ends.
Inputs may be any that keep to these rules, and one draw needn't show every extreme that they name: `expert_ids`: in the 128 rows of one device no expert is named more than 24 times. `log_decay`: negative. `write_strength`: positive.
All inputs are finite; a program needn't handle non-finite values.
Results may differ from the reference program's by a relative error of at most 0.011.
Values may be sent and summed in bfloat16 or wider, within the bound.
No kernel may reach another device: no remote copies, remote signals or barrier semaphores. Data moves between devices by JAX's collectives and lax.ppermute only.
A program may use at most 128 MiB of HBM per device.

```python
import math
import jax
import jax.numpy as jnp
import numpy as np
from jax import lax

D = 2048
VHEADS = 16
KHEADS = 8
HEAD = 128
FF = 512
SHARED_FF = 512
TOP = 10
SPAN = 64
TOK_DEV = 128
STREAM_LENGTH = 4096
EXPERTS = 64
CAP = 24


def head_plan(key):
    folded = jax.random.fold_in(key, 7)
    quick_heads = jax.random.uniform(folded, (VHEADS,)) < 0.5
    return quick_heads


def draw_log_decay(key, part):
    quick_heads = head_plan(key)
    stochastic_seeds = jax.random.split(jax.random.fold_in(key, 11), 6)
    quick_rates = jnp.exp(jax.random.uniform(stochastic_seeds[0], (VHEADS,), minval=jnp.log(1.0 / 50.0), maxval=jnp.log(1.0 / 30.0)))
    slow_rates = jnp.exp(jax.random.uniform(stochastic_seeds[1], (VHEADS,), minval=jnp.log(0.1), maxval=jnp.log(0.4))) / STREAM_LENGTH
    forgetting_speeds = jnp.where(quick_heads, quick_rates, slow_rates)
    jitter_scale = jax.random.uniform(stochastic_seeds[2], (STREAM_LENGTH, VHEADS), minval=0.5, maxval=1.5)
    segment_factor = jnp.exp(jax.random.uniform(stochastic_seeds[3], (STREAM_LENGTH // TOK_DEV, VHEADS), minval=jnp.log(0.5), maxval=jnp.log(2.0)))
    segment_factor = jnp.repeat(segment_factor, TOK_DEV, axis=0)
    spike_index = jax.random.randint(stochastic_seeds[4], (2,), 0, STREAM_LENGTH)
    magnitude_entries = jax.random.uniform(stochastic_seeds[5], (2, VHEADS), minval=0.22, maxval=0.69)
    element_index = jnp.arange(STREAM_LENGTH)[:, None]
    spike_indices = (element_index == spike_index[0]).astype(jnp.float32) * magnitude_entries[0][None, :]
    spike_indices = spike_indices + (element_index == spike_index[1]).astype(jnp.float32) * magnitude_entries[1][None, :]
    return (-(forgetting_speeds[None, :] * jitter_scale * segment_factor + spike_indices)).astype(jnp.float32)


def draw_write_strength(key, part):
    quick_heads = head_plan(key)
    stochastic_seeds = jax.random.split(jax.random.fold_in(key, 13), 3)
    quick_values = jax.random.uniform(stochastic_seeds[0], (STREAM_LENGTH, VHEADS), minval=0.05, maxval=0.95)
    slow_scale = jnp.exp(jax.random.uniform(stochastic_seeds[1], (VHEADS,), minval=jnp.log(0.25), maxval=0.0)) * HEAD / STREAM_LENGTH
    slow_values = slow_scale[None, :] * jax.random.uniform(stochastic_seeds[2], (STREAM_LENGTH, VHEADS), minval=0.5, maxval=1.5)
    return jnp.where(quick_heads[None, :], quick_values, slow_values).astype(jnp.float32)


def block_scale(key, dims, cuts, least, largest):
    factor_of, own = 1.0, jax.random.fold_in(key, 6)
    for dim, blocks in cuts:
        heights = jnp.exp(jax.random.uniform(jax.random.fold_in(own, dim), (blocks,), jnp.float32, least / len(cuts), largest / len(cuts)))
        factor_of = factor_of * jnp.repeat(heights, dims[dim] // blocks).reshape([-1 if axis == dim else 1 for axis in range(len(dims))])
    return factor_of


def assign_block(stream_key, own, number, rows, amount, top, bound, skew):
    order = jax.random.permutation(stream_key, amount)
    crowded, usual = portions_of(amount, rows * top, bound, skew, True), portions_of(amount, rows * top, bound, skew, False)
    places = jnp.arange(amount)

    def named(tallies, offset_by):
        used = int((tallies > 0).sum())
        fixed = max(1, used // 4)
        passed = fixed + (places - fixed + offset_by * (used - fixed)) % max(1, amount - fixed)
        return jnp.zeros((amount,), jnp.int32).at[order[jnp.where(places < fixed, places, passed)]].set(jnp.asarray(tallies, jnp.int32))

    tallies = jnp.where(number % 4 == 0, named(crowded, number // 4), named(usual, number - number // 4 - 1))
    mixed = jax.random.permutation(jax.random.fold_in(own, 3), amount)
    donor, receiver = mixed[0:amount // 2 * 2:2], mixed[1:amount // 2 * 2:2]
    room = jnp.minimum(tallies[donor] - 1, bound - tallies[receiver]) // 2
    room = jnp.where((donor == order[0]) | (receiver == order[0]) | (tallies[receiver] == 0), 0, jnp.maximum(room, 0))
    passed = jax.random.randint(jax.random.fold_in(own, 4), (amount // 2,), 0, 1 << 20) % (room + 1)
    tallies = tallies.at[donor].add(-passed).at[receiver].add(passed)
    items = jnp.searchsorted(jnp.cumsum(tallies), jnp.arange(rows * top), side="right").astype(jnp.int32)
    table = items.reshape(top, rows).T
    table = table[jax.random.permutation(jax.random.fold_in(own, 1), rows)]
    offset_by = jax.random.randint(jax.random.fold_in(own, 2), (rows, 1), 0, top)
    return jnp.take_along_axis(table, (jnp.arange(top)[None, :] + offset_by) % top, axis=1)


def portions_of(amount, total, reach, skew, full):
    loads = [(1 << 20) // math.isqrt(standing ** skew) + 1 for standing in range(1, amount + 1)]
    largest = reach if full else min(reach, max(-(-total // amount), total * loads[0] // sum(loads)))
    least = 1 if total - largest >= amount - 1 else 0
    counts, rest = [largest] + [least] * (amount - 1), total - largest - least * (amount - 1)
    while rest > 0:
        candidates = [i for i in range(1, amount) if counts[i] < largest] or [i for i in range(1, amount) if counts[i] < reach]
        pool, remaining = sum([loads[i] for i in candidates]), rest
        for i in candidates:
            more = min(reach - counts[i], max(1, remaining * loads[i] // pool), rest)
            counts[i] = counts[i] + more
            rest = rest - more
    return np.array(counts)


def normal_values(own_key, shape, deviation, bound, shards=(), kind=jnp.bfloat16):
    result = deviation * jax.random.normal(own_key, shape, jnp.float32)
    if shards:
        result = result * block_scale(own_key, shape, shards, -0.22, 0.18)
    return jnp.clip(result, -bound, bound).astype(kind)


def setup_inputs(seed: int = 0) -> dict:
    splits = jax.random.split(jax.random.key(seed), 19)
    residual = normal_values(splits[0], (STREAM_LENGTH, D), 1.0, 6.0, ((0, 32),))
    mixed_qkv = normal_values(splits[1], (STREAM_LENGTH, (2 * KHEADS + VHEADS) * HEAD), 1.0, 6.0, ((0, 32),))
    output_gate = normal_values(splits[2], (STREAM_LENGTH, VHEADS * HEAD), 1.0, 6.0, ((0, 32),))
    log_decay = draw_log_decay(jax.random.fold_in(splits[18], 71), 0)
    write_strength = draw_write_strength(jax.random.fold_in(splits[18], 71), 0)
    conv_weight = normal_values(splits[5], (4, (2 * KHEADS + VHEADS) * HEAD), 0.5, 3.0, (), jnp.float32)
    norm_gain = jnp.clip(1.0 + 0.18 * jax.random.normal(splits[6], (HEAD,), jnp.float32), 0.1, 1.9)
    out_weight = normal_values(splits[7], (VHEADS * HEAD, D), (VHEADS * HEAD) ** -0.5, 0.125, ((1, 4),))
    post_gain = jnp.clip(1.0 + 0.18 * jax.random.normal(splits[8], (D,), jnp.float32), 0.1, 1.9)
    router_weight = normal_values(splits[9], (D, EXPERTS), D ** -0.5, 0.125)
    expert_ids_keys = jax.random.split(jax.random.fold_in(splits[10], 1), STREAM_LENGTH // TOK_DEV)
    expert_ids_turns = jax.random.permutation(jax.random.fold_in(splits[10], 3), STREAM_LENGTH // TOK_DEV)
    expert_ids = jax.vmap(lambda own, number: assign_block(jax.random.fold_in(splits[10], 2), own, number, TOK_DEV, EXPERTS, TOP, CAP, 1))(expert_ids_keys, expert_ids_turns).reshape((STREAM_LENGTH, TOP))
    expert_gate = normal_values(splits[11], (EXPERTS, D, FF), D ** -0.5, 0.125, ((0, 32),))
    expert_up = normal_values(splits[12], (EXPERTS, D, FF), D ** -0.5, 0.125, ((0, 32),))
    expert_down = normal_values(splits[13], (EXPERTS, FF, D), FF ** -0.5, 0.25, ((0, 32),))
    shared_gate = normal_values(splits[14], (D, SHARED_FF), D ** -0.5, 0.125)
    shared_up = normal_values(splits[15], (D, SHARED_FF), D ** -0.5, 0.125)
    shared_down = normal_values(splits[16], (SHARED_FF, D), SHARED_FF ** -0.5, 0.25)
    shared_switch = normal_values(splits[17], (D,), D ** -0.5, 0.125)
    return dict(residual=residual, mixed_qkv=mixed_qkv, output_gate=output_gate, log_decay=log_decay, write_strength=write_strength, conv_weight=conv_weight, norm_gain=norm_gain, out_weight=out_weight, post_gain=post_gain, router_weight=router_weight, expert_ids=expert_ids, expert_gate=expert_gate, expert_up=expert_up, expert_down=expert_down, shared_gate=shared_gate, shared_up=shared_up, shared_down=shared_down, shared_switch=shared_switch)


highest_precision = lax.Precision.HIGHEST
epsilon = 1e-06

def short_conv(mixed_qkv, conv_weight, before):
    row_count = mixed_qkv.shape[0]
    padded = jnp.concatenate([before, mixed_qkv], axis=0).astype(jnp.float32)
    summed = conv_weight[3] * padded[3:3 + row_count]
    for tap_index in range(3):
        summed = summed + conv_weight[tap_index] * padded[tap_index:tap_index + row_count]
    return jax.nn.silu(summed)

def unit_rows(values_in):
    return values_in * lax.rsqrt(lax.optimization_barrier(jnp.sum(values_in * values_in, axis=-1, keepdims=True)) + epsilon)

def prepare(mixed_qkv, conv_weight, before):
    activated = short_conv(mixed_qkv, conv_weight, before)
    row_count = activated.shape[0]
    key_width = KHEADS * HEAD
    query_rows = unit_rows(activated[:, :key_width].reshape(row_count, KHEADS, HEAD)) * HEAD ** (-0.5)
    key_rows = unit_rows(activated[:, key_width:2 * key_width].reshape(row_count, KHEADS, HEAD))
    value_rows = activated[:, 2 * key_width:].reshape(row_count, VHEADS, HEAD)
    per_group = VHEADS // KHEADS
    query_rows = jnp.repeat(query_rows, per_group, axis=1)
    key_rows = jnp.repeat(key_rows, per_group, axis=1)
    return (query_rows.transpose(1, 0, 2), key_rows.transpose(1, 0, 2), value_rows.transpose(1, 0, 2))

def to_spans(head_rows):
    head_count, row_count, inner_width = head_rows.shape
    return head_rows.reshape(head_count, row_count // SPAN, SPAN, inner_width).transpose(1, 0, 2, 3)

def rates_to_spans(token_rates):
    row_count, head_count = token_rates.shape
    return token_rates.T.reshape(head_count, row_count // SPAN, SPAN).transpose(1, 0, 2)

def span_terms(query_rows, key_rows, value_rows, decay_rows, strength_rows):
    length = query_rows.shape[1]
    inner_width = key_rows.shape[2]
    cumul = jnp.cumsum(decay_rows, axis=1)
    causal = jnp.arange(length, dtype=jnp.int32)[:, None] >= jnp.arange(length, dtype=jnp.int32)[None, :]
    strict = jnp.arange(length, dtype=jnp.int32)[:, None] > jnp.arange(length, dtype=jnp.int32)[None, :]
    log_gap = cumul[:, :, None] - cumul[:, None, :]
    ratios = jnp.where(causal, jnp.exp(jnp.where(causal, log_gap, 0.0)), 0.0)
    key_inner = jnp.einsum('hck,hsk->hcs', key_rows, key_rows, precision=highest_precision)
    lower_part = jnp.where(strict, ratios * key_inner, 0.0) * strength_rows[:, :, None]
    system = jnp.eye(length, dtype=jnp.float32)[None] + lower_part
    decays = jnp.exp(cumul)
    right_operand = jnp.concatenate([strength_rows[:, :, None] * decays[:, :, None] * key_rows, strength_rows[:, :, None] * value_rows], axis=2)
    solved = jax.scipy.linalg.solve_triangular(system, right_operand, lower=True, unit_diagonal=True)
    key_weights = solved[:, :, :inner_width]
    fresh_values = solved[:, :, inner_width:]
    to_end = jnp.exp(cumul[:, -1:] - cumul)
    decayed_state = key_rows * to_end[:, :, None]
    identity = jnp.eye(inner_width, dtype=jnp.float32)[None]
    carry_transform = jnp.exp(cumul[:, -1])[:, None, None] * identity - jnp.einsum('hck,hcj->hkj', decayed_state, key_weights, precision=highest_precision)
    carry_offset = jnp.einsum('nae,nap->nep', decayed_state, fresh_values, precision=highest_precision)
    scores = jnp.einsum('hck,hsk->hcs', query_rows, key_rows, precision=highest_precision) * ratios
    read_transform = query_rows * decays[:, :, None] - jnp.einsum('hcs,hsk->hck', scores, key_weights, precision=highest_precision)
    read_offset = jnp.einsum('hcs,hsv->hcv', scores, fresh_values, precision=highest_precision)
    return (carry_transform, carry_offset, read_transform, read_offset)

def reference(residual, mixed_qkv, output_gate, log_decay, write_strength, conv_weight, norm_gain, out_weight, post_gain, router_weight, expert_ids, expert_gate, expert_up, expert_down, shared_gate, shared_up, shared_down, shared_switch):
    padding = jnp.zeros((3, mixed_qkv.shape[1]), mixed_qkv.dtype)
    query_rows, key_rows, value_rows = prepare(mixed_qkv, conv_weight, padding)
    span_inputs = (to_spans(query_rows), to_spans(key_rows), to_spans(value_rows), rates_to_spans(log_decay), rates_to_spans(write_strength))

    def advance(current_state, pieces):
        carry_transform, carry_offset, read_transform, read_offset = span_terms(*pieces)
        produced_output = jnp.einsum('urm,umn->urn', read_transform, current_state, precision=highest_precision) + read_offset
        following_state = jnp.einsum('coq,cqd->cod', carry_transform, current_state, precision=highest_precision) + carry_offset
        return (following_state, produced_output)
    start_state = jnp.zeros((VHEADS, HEAD, HEAD), jnp.float32)
    _, produced_output = lax.scan(advance, start_state, span_inputs)
    mixer_out = produced_output.transpose(0, 2, 1, 3).reshape(STREAM_LENGTH, VHEADS, HEAD)
    gate_rows = output_gate.reshape(STREAM_LENGTH, VHEADS, HEAD).astype(jnp.float32)
    normed = mixer_out * lax.rsqrt(lax.optimization_barrier(jnp.mean(mixer_out * mixer_out, axis=-1, keepdims=True)) + epsilon)
    normed = (normed * norm_gain * jax.nn.silu(gate_rows)).reshape(STREAM_LENGTH, VHEADS * HEAD).astype(jnp.bfloat16)
    after_mix = (residual.astype(jnp.float32) + jnp.dot(normed.astype(jnp.float32), out_weight.astype(jnp.float32), preferred_element_type=jnp.float32)).astype(jnp.bfloat16)
    after_wide = after_mix.astype(jnp.float32)
    routed_in = (after_wide * lax.rsqrt(lax.optimization_barrier(jnp.mean(after_wide * after_wide, axis=-1, keepdims=True)) + epsilon) * post_gain).astype(jnp.bfloat16)
    logits = jnp.dot(routed_in.astype(jnp.float32), router_weight.astype(jnp.float32), preferred_element_type=jnp.float32)
    chosen = jnp.exp(jnp.take_along_axis(logits, expert_ids, axis=1))
    gate_weights = chosen / lax.optimization_barrier(jnp.sum(chosen, axis=1, keepdims=True))
    shared_hidden = (jax.nn.silu(jnp.dot(routed_in.astype(jnp.float32), shared_gate.astype(jnp.float32), preferred_element_type=jnp.float32)) * jnp.dot(routed_in.astype(jnp.float32), shared_up.astype(jnp.float32), preferred_element_type=jnp.float32)).astype(jnp.bfloat16)
    switch_rows = jax.nn.sigmoid(jnp.dot(routed_in.astype(jnp.float32), shared_switch.astype(jnp.float32), preferred_element_type=jnp.float32))
    shared_out = switch_rows[:, None] * jnp.dot(shared_hidden.astype(jnp.float32), shared_down.astype(jnp.float32), preferred_element_type=jnp.float32)
    block_count = STREAM_LENGTH // TOK_DEV
    flat_ids = expert_ids.reshape(block_count, TOK_DEV * TOP)

    def ranks_of(row_ids):
        onehot = (row_ids[:, None] == jnp.arange(EXPERTS, dtype=jnp.int32)[None, :]).astype(jnp.int32)
        earlier = jnp.cumsum(onehot, axis=0) - onehot
        return lax.optimization_barrier(jnp.sum(earlier * onehot, axis=1)).astype(jnp.int32)
    slot_rank = lax.map(ranks_of, flat_ids)
    block_of = jnp.broadcast_to(jnp.arange(block_count, dtype=jnp.int32)[:, None], flat_ids.shape)
    token_of = block_of * TOK_DEV + jnp.arange(TOK_DEV * TOP, dtype=jnp.int32)[None, :] // TOP
    rows_table = jnp.zeros((EXPERTS, block_count, CAP), jnp.int32).at[flat_ids, block_of, slot_rank].set(token_of)
    scale_table = jnp.zeros((EXPERTS, block_count, CAP), jnp.float32).at[flat_ids, block_of, slot_rank].set(gate_weights.reshape(block_count, TOK_DEV * TOP))

    def expert_step(accumulated, pieces):
        row_ids, slot_scale, gate_w, up_w, down_w = pieces
        row_ids = row_ids.reshape(-1)
        slot_scale = slot_scale.reshape(-1)
        taken_rows = routed_in[row_ids]
        expert_hidden = (jax.nn.silu(jnp.dot(taken_rows.astype(jnp.float32), gate_w.astype(jnp.float32), preferred_element_type=jnp.float32)) * jnp.dot(taken_rows.astype(jnp.float32), up_w.astype(jnp.float32), preferred_element_type=jnp.float32)).astype(jnp.bfloat16)
        expert_out = jnp.dot(expert_hidden.astype(jnp.float32), down_w.astype(jnp.float32), preferred_element_type=jnp.float32).astype(jnp.bfloat16)
        return (accumulated.at[row_ids].add(expert_out.astype(jnp.float32) * slot_scale[:, None]), None)
    routed, _ = lax.scan(expert_step, jnp.zeros((STREAM_LENGTH, D), jnp.float32), (rows_table, scale_table, expert_gate, expert_up, expert_down))
    return (after_mix.astype(jnp.float32) + routed + shared_out).astype(jnp.bfloat16)
```

```python
import functools

import jax
import jax.numpy as jnp
from jax import lax
from jax.experimental import pallas as pl
from jax.experimental.pallas import tpu as pltpu
from jax.sharding import PartitionSpec as P

AXES = ("ctx", "exp")
EPS = 1e-06
F32, BF16 = jnp.float32, jnp.bfloat16


def dot(a, b, dims=((1,), (0,))):
    return lax.dot_general(a, b, (dims, ((), ())), preferred_element_type=F32)


def halves(x):
    hi = x.astype(BF16)
    return hi, (x - hi.astype(F32)).astype(BF16)


def dot_square(a, b):
    n = b.shape[1]
    ah, al = halves(a)
    bh, bl = halves(b)
    left = jnp.concatenate([ah, al], axis=1)
    right = jnp.concatenate(
        [jnp.concatenate([bh, bl], axis=1), jnp.concatenate([bh, jnp.zeros_like(bl)], axis=1)], axis=0
    )
    both = dot(left, right)
    return both[:, :n] + both[:, n:]


def dot_wide(a, b):
    ah, al = halves(a)
    bh, bl = halves(b)
    return dot(jnp.concatenate([ah, al], axis=1), jnp.concatenate([bh, bh], axis=0)) + dot(ah, bl)


def unit_lower_inverse(lower):
    n = lower[0].shape[0]
    row = lax.broadcasted_iota(jnp.int32, (n, n), 0)
    col = lax.broadcasted_iota(jnp.int32, (n, n), 1)
    eye = jnp.where(row == col, 1.0, 0.0)
    size = 1
    done = None
    while size < n:
        pair = (row // (2 * size) == col // (2 * size)) & (row // size != col // size)
        corner = [jnp.where(pair, m, 0.0) for m in lower]
        if size == 1:
            done = [eye - c for c in corner]
        else:
            half = [dot_square(d, c) for d, c in zip(done, corner)]
            done = [d - dot_square(h, d) for d, h in zip(done, half)]
        size *= 2
    return done


def delta_kernel(q_ref, k_ref, v_ref, qb_ref, kb_ref, vb_ref, qw_ref, kw_ref, vw_ref, cols_ref, rows_ref, map_ref, read_ref, *, head, per):
    rows = q_ref.shape[0]
    groups = q_ref.shape[1] // head

    def conv(x_ref, b_ref, w_ref):
        x = jnp.concatenate([b_ref[...].astype(F32), x_ref[...].astype(F32)], axis=0)
        w = w_ref[...]
        y = w[3:4] * x[8 : 8 + rows]
        for tap in range(3):
            y = y + w[tap : tap + 1] * x[5 + tap : 5 + tap + rows]
        return y / (1.0 + jnp.exp(-y))

    def unit(x):
        return x * lax.rsqrt(jnp.sum(x * x, axis=-1, keepdims=True) + EPS)

    q_all, k_all, v_all = conv(q_ref, qb_ref, qw_ref), conv(k_ref, kb_ref, kw_ref), conv(v_ref, vb_ref, vw_ref)
    row = lax.broadcasted_iota(jnp.int32, (rows, rows), 0)
    col = lax.broadcasted_iota(jnp.int32, (rows, rows), 1)
    lower, info = [], []
    for g in range(groups):
        q = unit(q_all[:, g * head : (g + 1) * head]) * head**-0.5
        k = unit(k_all[:, g * head : (g + 1) * head])
        kh, kl = halves(k)
        qh, ql = halves(q)
        top = jnp.concatenate([jnp.concatenate([kh, kl], axis=1), jnp.concatenate([qh, ql], axis=1)], axis=0)
        inner = dot(top, jnp.concatenate([kh, kh], axis=1), ((1,), (1,)))
        inner = inner + dot(jnp.concatenate([kh, qh], axis=0), kl, ((1,), (1,)))
        kk, qk = inner[:rows], inner[rows:]
        for i in range(per):
            j = g * per + i
            cum_col = cols_ref[j, :, 0:1]
            strength = cols_ref[j, :, 1:2]
            cum_row = rows_ref[j, 0:1, :]
            gap = cum_col - cum_row
            ratios = jnp.where(row >= col, jnp.exp(jnp.where(row >= col, gap, 0.0)), 0.0)
            lower.append(jnp.where(row > col, ratios * kk, 0.0) * strength)
            info.append((q, k, v_all[:, j * head : (j + 1) * head], cum_col, strength, qk * ratios))
    inverse = unit_lower_inverse(lower)
    for j, (q, k, v, cum, strength, scores) in enumerate(info):
        decay = jnp.exp(cum)
        right = jnp.concatenate([strength * decay * k, strength * v], axis=1)
        solved = dot_wide(inverse[j], right)
        last = cum[rows - 1 : rows]
        to_end = k * jnp.exp(last - cum)
        update = dot_wide(to_end.T, solved)
        end = jnp.exp(last)
        diag = lax.broadcasted_iota(jnp.int32, (head, head), 0) == lax.broadcasted_iota(jnp.int32, (head, head), 1)
        map_ref[j, :, :head] = jnp.where(diag, end, 0.0) - update[:, :head]
        map_ref[j, :, head:] = update[:, head:]
        read = dot_wide(scores, solved)
        read_ref[j, :, :head] = q * decay - read[:, :head]
        read_ref[j, :, head:] = read[:, head:]


def delta_terms(mixed, before, conv_weight, log_decay, write_strength, head):
    rows, vheads = log_decay.shape
    kheads = (mixed.shape[1] // head - vheads) // 2
    per = vheads // kheads
    together = 2 if kheads % 2 == 0 else 1
    steps = kheads // together
    causal = jnp.tril(jnp.ones((rows, rows), F32))
    cumul = jnp.dot(causal, log_decay, precision=lax.Precision.HIGHEST)
    cols = jnp.stack([cumul.T, write_strength.T], axis=2)
    lines = cumul.T[:, None, :]
    qw, vw = together * head, together * per * head
    k_at, v_at = kheads * head // qw, 2 * kheads * head // vw

    def spec(height, width, at):
        return pl.BlockSpec((height, width), lambda s: (0, s + at))

    n = together * per
    return pl.pallas_call(
        functools.partial(delta_kernel, head=head, per=per),
        grid=(steps,),
        in_specs=[spec(h, w, a) for h in (rows, 8, 4) for w, a in ((qw, 0), (qw, k_at), (vw, v_at))]
        + [
            pl.BlockSpec((n, rows, 2), lambda s: (s, 0, 0)),
            pl.BlockSpec((n, 1, rows), lambda s: (s, 0, 0)),
        ],
        out_specs=[pl.BlockSpec((n, head, 2 * head), lambda s: (s, 0, 0)), pl.BlockSpec((n, rows, 2 * head), lambda s: (s, 0, 0))],
        out_shape=[jax.ShapeDtypeStruct((vheads, head, 2 * head), F32), jax.ShapeDtypeStruct((vheads, rows, 2 * head), F32)],
        compiler_params=pltpu.CompilerParams(vmem_limit_bytes=40 * 2**20),
        name="delta_terms",
    )(mixed, mixed, mixed, before, before, before, conv_weight, conv_weight, conv_weight, cols, lines)


def emit_kernel(read_ref, state_ref, gate_ref, gain_ref, out_ref):
    n, rows, head2 = read_ref.shape
    head = head2 // 2
    for j in range(n):
        out = dot_square(read_ref[j, :, :head], state_ref[j]) + read_ref[j, :, head:]
        normed = out * lax.rsqrt(jnp.mean(out * out, axis=-1, keepdims=True) + EPS)
        gate = gate_ref[:, j * head : (j + 1) * head].astype(F32)
        out_ref[:, j * head : (j + 1) * head] = (normed * gain_ref[...] * (gate / (1.0 + jnp.exp(-gate)))).astype(BF16)


def emit(read, state, output_gate, gain):
    vheads, rows, head2 = read.shape
    head = head2 // 2
    n = 4 if vheads % 4 == 0 else 1
    return pl.pallas_call(
        emit_kernel,
        grid=(vheads // n,),
        in_specs=[
            pl.BlockSpec((n, rows, head2), lambda s: (s, 0, 0)),
            pl.BlockSpec((n, head, head), lambda s: (s, 0, 0)),
            pl.BlockSpec((rows, n * head), lambda s: (0, s)),
            pl.BlockSpec((1, head), lambda s: (0, 0)),
        ],
        out_specs=pl.BlockSpec((rows, n * head), lambda s: (0, s)),
        out_shape=jax.ShapeDtypeStruct((rows, vheads * head), BF16),
        name="emit",
    )(read, state, output_gate, gain[None])


def apply(transform, right):
    return jnp.einsum("hij,hjk->hik", transform, right, precision=lax.Precision.HIGHEST)


def starting_states(block_map, count, place):
    head = block_map.shape[1]
    levels, step = [], 1
    held = block_map
    while count % (2 * step) == 0 and 4 * step < count and held.shape[0] % 2 == 0:
        share = held.shape[0] // 2
        upper = (place // step) % 2 == 1
        keep = jnp.where(upper, held[share:], held[:share])
        give = jnp.where(upper, held[:share], held[share:])
        got = lax.ppermute(give, AXES, [(i, i ^ step) for i in range(count)])
        early, late = jnp.where(upper, got, keep), jnp.where(upper, keep, got)
        merged = apply(late[:, :, :head], early)
        held = jnp.concatenate([merged[:, :, :head], merged[:, :, head:] + late[:, :, head:]], axis=2)
        levels.append((step, upper, early))
        step *= 2
    state = jnp.zeros_like(held[:, :, head:])
    for turn in range(count // step - 1):
        ahead = held[:, :, head:]
        if turn:
            ahead = ahead + apply(held[:, :, :head], state)
        state = lax.ppermute(ahead, AXES, [(i, i + step) for i in range(count - step)])
    for step, upper, early in reversed(levels):
        second = apply(early[:, :, :head], state) + early[:, :, head:]
        mine, other = jnp.where(upper, second, state), jnp.where(upper, state, second)
        got = lax.ppermute(other, AXES, [(i, i ^ step) for i in range(count)])
        state = jnp.where(upper, jnp.concatenate([got, mine], axis=0), jnp.concatenate([mine, got], axis=0))
    return state


def local(
    residual,
    mixed_qkv,
    output_gate,
    log_decay,
    write_strength,
    conv_weight,
    norm_gain,
    out_weight,
    post_gain,
    router_weight,
    expert_ids,
    expert_gate,
    expert_up,
    expert_down,
    shared_gate,
    shared_up,
    shared_down,
    shared_switch,
):
    rows, width = residual.shape
    head = norm_gain.shape[0]
    count = lax.axis_size(AXES)
    place = lax.axis_index(AXES)
    before = lax.ppermute(mixed_qkv[rows - 8 :], AXES, [(i, i + 1) for i in range(count - 1)])
    block_map, read = delta_terms(mixed_qkv, before, conv_weight, log_decay, write_strength, head)
    state = starting_states(block_map, count, place)
    normed = emit(read, state, output_gate, norm_gain)
    projected = jnp.dot(normed, lax.all_gather(out_weight, "exp", axis=1, tiled=True), preferred_element_type=F32)
    after_mix = (residual.astype(F32) + projected).astype(BF16)
    after_wide = after_mix.astype(F32)
    routed_in = (
        after_wide * lax.rsqrt(jnp.mean(after_wide * after_wide, axis=-1, keepdims=True) + EPS) * post_gain
    ).astype(BF16)

    local_count = expert_gate.shape[0]
    experts = local_count * count
    top = expert_ids.shape[1]
    capacity = rows * top * 6 // (experts * 5)
    named = jnp.any(expert_ids[:, :, None] == jnp.arange(experts, dtype=jnp.int32), axis=1)
    earlier = jnp.dot(jnp.tril(jnp.ones((rows, rows), BF16), -1), named.astype(BF16), preferred_element_type=F32)
    slot = jnp.where(named, earlier.astype(jnp.int32), capacity)
    picks = (slot.T[:, None, :] == jnp.arange(capacity, dtype=jnp.int32)[None, :, None]).reshape(experts * capacity, rows)

    logits = jnp.dot(routed_in, router_weight, preferred_element_type=F32)
    chosen = jnp.where(named, jnp.exp(jnp.where(named, logits, 0.0)), 0.0)
    gates = chosen / jnp.sum(chosen, axis=1, keepdims=True)
    outgoing = jnp.dot(picks.astype(BF16), routed_in, preferred_element_type=F32).astype(BF16)
    received = lax.all_to_all(
        outgoing.reshape(count, local_count, capacity, width), AXES, split_axis=0, concat_axis=0, tiled=True
    )
    shared_hidden = (
        jax.nn.silu(jnp.dot(routed_in, shared_gate, preferred_element_type=F32))
        * jnp.dot(routed_in, shared_up, preferred_element_type=F32)
    ).astype(BF16)
    switch = jax.nn.sigmoid(jnp.dot(routed_in, shared_switch, preferred_element_type=F32))
    shared_out = switch[:, None] * jnp.dot(shared_hidden, shared_down, preferred_element_type=F32)

    received = received.transpose(1, 0, 2, 3).reshape(local_count, count * capacity, width)
    gate_part = jnp.einsum("esd,edf->esf", received, expert_gate, preferred_element_type=F32)
    up_part = jnp.einsum("esd,edf->esf", received, expert_up, preferred_element_type=F32)
    hidden = (jax.nn.silu(gate_part) * up_part).astype(BF16)
    result = jnp.einsum("esf,efd->esd", hidden, expert_down, preferred_element_type=F32).astype(BF16)
    result = result.reshape(local_count, count, capacity, width).transpose(1, 0, 2, 3)
    returned = lax.all_to_all(result, AXES, split_axis=0, concat_axis=0, tiled=True)
    spread = jnp.where(slot[:, :, None] == jnp.arange(capacity, dtype=jnp.int32), gates[:, :, None], 0.0)
    spread_hi, spread_lo = halves(spread.reshape(rows, experts * capacity))
    pulled = jnp.dot(
        jnp.concatenate([spread_hi, spread_lo], axis=0),
        returned.reshape(experts * capacity, width),
        preferred_element_type=F32,
    )
    return (after_wide + pulled[:rows] + pulled[rows:] + shared_out).astype(BF16)


def solution(mesh):
    rows = P(AXES, None)
    return jax.shard_map(
        local,
        mesh=mesh,
        in_specs=(rows, rows, rows, rows, rows, P(), P(), P(None, "exp"), P(), P(), rows)
        + (P(AXES, None, None),) * 3
        + (P(),) * 4,
        out_specs=rows,
        check_vma=False,
    )
```

```python
import functools

import jax
import jax.numpy as jnp
from jax import lax
from jax.experimental import pallas as pl
from jax.experimental.pallas import tpu as pltpu
from jax.sharding import PartitionSpec as P

AXES = ("ctx", "exp")
EPS = 1e-06
F32, BF16 = jnp.float32, jnp.bfloat16


def dot(a, b, dims=((1,), (0,))):
    return lax.dot_general(a, b, (dims, ((), ())), preferred_element_type=F32)


def halves(x):
    hi = x.astype(BF16)
    return hi, (x - hi.astype(F32)).astype(BF16)


def dot_square(a, b):
    n = b.shape[1]
    ah, al = halves(a)
    bh, bl = halves(b)
    left = jnp.concatenate([ah, al], axis=1)
    right = jnp.concatenate(
        [jnp.concatenate([bh, bl], axis=1), jnp.concatenate([bh, jnp.zeros_like(bl)], axis=1)], axis=0
    )
    both = dot(left, right)
    return both[:, :n] + both[:, n:]


def dot_wide(a, b):
    ah, al = halves(a)
    bh, bl = halves(b)
    return dot(jnp.concatenate([ah, al], axis=1), jnp.concatenate([bh, bh], axis=0)) + dot(ah, bl)


def unit_lower_inverse(lower):
    n = lower[0].shape[0]
    row = lax.broadcasted_iota(jnp.int32, (n, n), 0)
    col = lax.broadcasted_iota(jnp.int32, (n, n), 1)
    eye = jnp.where(row == col, 1.0, 0.0)
    size = 1
    done = None
    while size < n:
        pair = (row // (2 * size) == col // (2 * size)) & (row // size != col // size)
        corner = [jnp.where(pair, m, 0.0) for m in lower]
        if size == 1:
            done = [eye - c for c in corner]
        else:
            half = [dot_square(d, c) for d, c in zip(done, corner)]
            done = [d - dot_square(h, d) for d, h in zip(done, half)]
        size *= 2
    return done


def delta_kernel(q_ref, k_ref, v_ref, qb_ref, kb_ref, vb_ref, qw_ref, kw_ref, vw_ref, cols_ref, rows_ref, map_ref, read_ref, *, head, per):
    rows = q_ref.shape[0]
    groups = q_ref.shape[1] // head

    def conv(x_ref, b_ref, w_ref):
        x = jnp.concatenate([b_ref[...].astype(F32), x_ref[...].astype(F32)], axis=0)
        w = w_ref[...]
        y = w[3:4] * x[8 : 8 + rows]
        for tap in range(3):
            y = y + w[tap : tap + 1] * x[5 + tap : 5 + tap + rows]
        return y / (1.0 + jnp.exp(-y))

    def unit(x):
        return x * lax.rsqrt(jnp.sum(x * x, axis=-1, keepdims=True) + EPS)

    q_all, k_all, v_all = conv(q_ref, qb_ref, qw_ref), conv(k_ref, kb_ref, kw_ref), conv(v_ref, vb_ref, vw_ref)
    row = lax.broadcasted_iota(jnp.int32, (rows, rows), 0)
    col = lax.broadcasted_iota(jnp.int32, (rows, rows), 1)
    lower, info = [], []
    for g in range(groups):
        q = unit(q_all[:, g * head : (g + 1) * head]) * head**-0.5
        k = unit(k_all[:, g * head : (g + 1) * head])
        kh, kl = halves(k)
        qh, ql = halves(q)
        top = jnp.concatenate([jnp.concatenate([kh, kl], axis=1), jnp.concatenate([qh, ql], axis=1)], axis=0)
        inner = dot(top, jnp.concatenate([kh, kh], axis=1), ((1,), (1,)))
        inner = inner + dot(jnp.concatenate([kh, qh], axis=0), kl, ((1,), (1,)))
        kk, qk = inner[:rows], inner[rows:]
        for i in range(per):
            j = g * per + i
            cum_col = cols_ref[j, :, 0:1]
            strength = cols_ref[j, :, 1:2]
            cum_row = rows_ref[j, 0:1, :]
            gap = cum_col - cum_row
            ratios = jnp.where(row >= col, jnp.exp(jnp.where(row >= col, gap, 0.0)), 0.0)
            lower.append(jnp.where(row > col, ratios * kk, 0.0) * strength)
            info.append((q, k, v_all[:, j * head : (j + 1) * head], cum_col, strength, qk * ratios))
    inverse = unit_lower_inverse(lower)
    for j, (q, k, v, cum, strength, scores) in enumerate(info):
        decay = jnp.exp(cum)
        right = jnp.concatenate([strength * decay * k, strength * v], axis=1)
        solved = dot_wide(inverse[j], right)
        last = cum[rows - 1 : rows]
        to_end = k * jnp.exp(last - cum)
        update = dot_wide(to_end.T, solved)
        end = jnp.exp(last)
        diag = lax.broadcasted_iota(jnp.int32, (head, head), 0) == lax.broadcasted_iota(jnp.int32, (head, head), 1)
        map_ref[j, :, :head] = jnp.where(diag, end, 0.0) - update[:, :head]
        map_ref[j, :, head:] = update[:, head:]
        read = dot_wide(scores, solved)
        read_ref[j, :, :head] = q * decay - read[:, :head]
        read_ref[j, :, head:] = read[:, head:]


def delta_terms(mixed, before, conv_weight, log_decay, write_strength, head):
    rows, vheads = log_decay.shape
    kheads = (mixed.shape[1] // head - vheads) // 2
    per = vheads // kheads
    together = 2 if kheads % 2 == 0 else 1
    steps = kheads // together
    causal = jnp.tril(jnp.ones((rows, rows), F32))
    cumul = jnp.dot(causal, log_decay, precision=lax.Precision.HIGHEST)
    cols = jnp.stack([cumul.T, write_strength.T], axis=2)
    lines = cumul.T[:, None, :]
    qw, vw = together * head, together * per * head
    k_at, v_at = kheads * head // qw, 2 * kheads * head // vw

    def spec(height, width, at):
        return pl.BlockSpec((height, width), lambda s: (0, s + at))

    n = together * per
    return pl.pallas_call(
        functools.partial(delta_kernel, head=head, per=per),
        grid=(steps,),
        in_specs=[spec(h, w, a) for h in (rows, 8, 4) for w, a in ((qw, 0), (qw, k_at), (vw, v_at))]
        + [
            pl.BlockSpec((n, rows, 2), lambda s: (s, 0, 0)),
            pl.BlockSpec((n, 1, rows), lambda s: (s, 0, 0)),
        ],
        out_specs=[pl.BlockSpec((n, head, 2 * head), lambda s: (s, 0, 0)), pl.BlockSpec((n, rows, 2 * head), lambda s: (s, 0, 0))],
        out_shape=[jax.ShapeDtypeStruct((vheads, head, 2 * head), F32), jax.ShapeDtypeStruct((vheads, rows, 2 * head), F32)],
        compiler_params=pltpu.CompilerParams(vmem_limit_bytes=40 * 2**20),
        name="delta_terms",
    )(mixed, mixed, mixed, before, before, before, conv_weight, conv_weight, conv_weight, cols, lines)


def emit_kernel(read_ref, state_ref, gate_ref, gain_ref, out_ref):
    n, rows, head2 = read_ref.shape
    head = head2 // 2
    for j in range(n):
        out = dot_square(read_ref[j, :, :head], state_ref[j]) + read_ref[j, :, head:]
        normed = out * lax.rsqrt(jnp.mean(out * out, axis=-1, keepdims=True) + EPS)
        gate = gate_ref[:, j * head : (j + 1) * head].astype(F32)
        out_ref[:, j * head : (j + 1) * head] = (normed * gain_ref[...] * (gate / (1.0 + jnp.exp(-gate)))).astype(BF16)


def emit(read, state, output_gate, gain):
    vheads, rows, head2 = read.shape
    head = head2 // 2
    n = 4 if vheads % 4 == 0 else 1
    return pl.pallas_call(
        emit_kernel,
        grid=(vheads // n,),
        in_specs=[
            pl.BlockSpec((n, rows, head2), lambda s: (s, 0, 0)),
            pl.BlockSpec((n, head, head), lambda s: (s, 0, 0)),
            pl.BlockSpec((rows, n * head), lambda s: (0, s)),
            pl.BlockSpec((1, head), lambda s: (0, 0)),
        ],
        out_specs=pl.BlockSpec((rows, n * head), lambda s: (0, s)),
        out_shape=jax.ShapeDtypeStruct((rows, vheads * head), BF16),
        name="emit",
    )(read, state, output_gate, gain[None])


def apply(transform, right):
    return jnp.einsum("hij,hjk->hik", transform, right, precision=lax.Precision.HIGHEST)


def starting_states(block_map, count, place):
    head = block_map.shape[1]
    levels, step = [], 1
    held = block_map
    while count % (2 * step) == 0 and 4 * step < count and held.shape[0] % 2 == 0:
        share = held.shape[0] // 2
        upper = (place // step) % 2 == 1
        keep = jnp.where(upper, held[share:], held[:share])
        give = jnp.where(upper, held[:share], held[share:])
        kind = F32 if step == 1 else BF16
        got = lax.ppermute(give.astype(kind), AXES, [(i, i ^ step) for i in range(count)]).astype(F32)
        early, late = jnp.where(upper, got, keep), jnp.where(upper, keep, got)
        merged = apply(late[:, :, :head], early)
        held = jnp.concatenate([merged[:, :, :head], merged[:, :, head:] + late[:, :, head:]], axis=2)
        levels.append((step, upper, early))
        step *= 2
    state = jnp.zeros_like(held[:, :, head:])
    for turn in range(count // step - 1):
        ahead = held[:, :, head:]
        if turn:
            ahead = ahead + apply(held[:, :, :head], state)
        state = lax.ppermute(ahead.astype(BF16), AXES, [(i, i + step) for i in range(count - step)]).astype(F32)
    for step, upper, early in reversed(levels):
        second = apply(early[:, :, :head], state) + early[:, :, head:]
        mine, other = jnp.where(upper, second, state), jnp.where(upper, state, second)
        got = lax.ppermute(other.astype(BF16), AXES, [(i, i ^ step) for i in range(count)]).astype(F32)
        state = jnp.where(upper, jnp.concatenate([got, mine], axis=0), jnp.concatenate([mine, got], axis=0))
    return state


def places(mesh):
    at = {(*d.coords, d.core_on_chip): i for i, d in enumerate(mesh.devices.flat)}
    return at, tuple(max(c[k] for c in at) + 1 for k in range(4))


def moves(layout, x=0, y=0, z=0, core=0):
    at, size = layout
    shift = (x, y, z, core)
    return [(i, at[tuple((c + s) % n for c, s, n in zip(spot, shift, size))]) for spot, i in at.items()]


def expert_kernel(*refs, width, capacity, local_count):
    shards, (chosen_ref, *weights), outs = refs[:8], refs[8:15], refs[15:23]
    sel_ref, pick_ref, gate_ref, back_ref = refs[23:]
    step = pl.program_id(0)
    steps = 2 * local_count
    rows = shards[0].shape[0]
    pair_rows, slots = 2 * rows, 2 * capacity
    tile = width // 4
    pairs = [(shards[i], shards[i + 1]) for i in range(0, 8, 2)]

    def read(pair, lo, hi):
        return jnp.concatenate([r[:, lo:hi] for r in pair], axis=0)

    @pl.when(step == 0)
    def _():
        before = lax.broadcasted_iota(jnp.int32, (pair_rows, pair_rows), 0)
        after = lax.broadcasted_iota(jnp.int32, (pair_rows, pair_rows), 1)
        earlier = jnp.where((before < after) & (before // rows == after // rows), 1.0, 0.0).astype(BF16)
        second = lax.broadcasted_iota(jnp.int32, (1, pair_rows), 1) // rows
        slot = lax.broadcasted_iota(jnp.int32, (slots, pair_rows), 0)
        for p, pair in enumerate(pairs):
            gates = dot(chosen_ref[...], read(pair, width, pair[0].shape[1]), ((1,), (1,)))
            named = jnp.where(gates != 0.0, 1.0, 0.0)
            rank = dot(named.astype(BF16), earlier).astype(jnp.int32)
            spot = jnp.where(gates != 0.0, rank + second * capacity, -1)
            for e in range(steps):
                hit = slot == spot[e : e + 1]
                pick_ref[p, e * slots : (e + 1) * slots, :] = jnp.where(hit, 1.0, 0.0).astype(BF16)
                gate = jnp.sum(jnp.where(hit, gates[e : e + 1], 0.0), axis=1, keepdims=True)
                gate_ref[e, p * slots : (p + 1) * slots, :] = jnp.broadcast_to(gate, (slots, 128))
            for n in range(4):
                taken = dot(pick_ref[p], read(pair, n * tile, (n + 1) * tile)).astype(BF16)
                for e in range(steps):
                    sel_ref[e, p * slots : (p + 1) * slots, n * tile : (n + 1) * tile] = taken[e * slots : (e + 1) * slots]

    def run(g_ref, u_ref, d_ref):
        rows_in = sel_ref[step]
        gate, up = dot(rows_in, g_ref[0]), dot(rows_in, u_ref[0])
        hidden = (gate / (1.0 + jnp.exp(-gate)) * up).astype(BF16)
        weight = gate_ref[step][:, 0:1]
        at = pl.multiple_of(step * slots, slots)
        for n in range(4):
            result = (dot(hidden, d_ref[0, :, n * tile : (n + 1) * tile]) * weight).astype(BF16)
            for p in range(len(pairs)):
                back_ref[p, pl.ds(at, slots), n * tile : (n + 1) * tile] = result[p * slots : (p + 1) * slots]

    @pl.when(step < local_count)
    def _():
        run(*weights[:3])

    @pl.when(step >= local_count)
    def _():
        run(*weights[3:])

    @pl.when(step == steps - 1)
    def _():
        for p in range(len(pairs)):
            spread = pick_ref[p].astype(F32).T.astype(BF16)
            for n in range(4):
                cut = slice(n * tile, (n + 1) * tile)
                total = dot(spread, back_ref[p, :, cut]).astype(BF16)
                outs[2 * p][:, cut] = total[:rows]
                outs[2 * p + 1][:, cut] = total[rows:]


def run_experts(shards, chosen, mine, other, width, capacity):
    local_count, _, hidden = mine[0].shape
    steps = 2 * local_count
    slots = 2 * capacity
    rows = shards[0].shape[0]
    whole = lambda a: pl.BlockSpec(a.shape, lambda s: (0,) * a.ndim)
    first = lambda a: pl.BlockSpec((1, *a.shape[1:]), lambda s: (jnp.minimum(s, local_count - 1), 0, 0))
    then = lambda a: pl.BlockSpec((1, *a.shape[1:]), lambda s: (jnp.maximum(s - local_count, 0), 0, 0))
    shapes = [jax.ShapeDtypeStruct((rows, width), BF16)] * 8
    return pl.pallas_call(
        functools.partial(expert_kernel, width=width, capacity=capacity, local_count=local_count),
        grid=(steps,),
        in_specs=[whole(a) for a in (*shards, chosen)] + [first(a) for a in mine] + [then(a) for a in other],
        out_specs=[whole(a) for a in shapes],
        out_shape=shapes,
        scratch_shapes=[
            pltpu.VMEM((steps, 4 * slots, width), BF16),
            pltpu.VMEM((4, steps * slots, 2 * rows), BF16),
            pltpu.VMEM((steps, 4 * slots, 128), F32),
            pltpu.VMEM((4, steps * slots, width), BF16),
        ],
        cost_estimate=pl.CostEstimate(
            flops=steps * 4 * slots * (6 * width * hidden + 8 * width * rows),
            bytes_accessed=6 * width * hidden * steps + 32 * rows * width,
            transcendentals=0,
        ),
        compiler_params=pltpu.CompilerParams(vmem_limit_bytes=58 * 2**20),
        name="experts",
    )(*shards, chosen, *mine, *other)


def tie(value, *after):
    return lax.optimization_barrier((value, *after))[0]


def plus(*parts):
    return sum(p.astype(F32) for p in parts[1:]) + parts[0].astype(F32)


def routed_by_gather(layout, place, routed_in, gates, weights, other, capacity):
    rows, width = routed_in.shape
    experts = gates.shape[1]
    local_count = weights[0].shape[0]
    deep = layout[1][2]
    send = lambda a, **by: lax.ppermute(a, AXES, moves(layout, **by))
    partner = jnp.asarray([j for _, j in sorted(moves(layout, core=1))], jnp.int32)[place]
    ids = jnp.concatenate([p * local_count + jnp.arange(local_count, dtype=jnp.int32) for p in (place, partner)])
    ids = jnp.pad(ids, (0, -ids.shape[0] % 8), constant_values=experts)
    chosen = (ids[:, None] == jnp.arange(experts, dtype=jnp.int32)).astype(BF16)
    pad = -(2 * experts) % 128
    chosen = jnp.pad(jnp.concatenate([chosen, chosen], axis=1), ((0, 0), (0, pad)))
    gates_hi, gates_lo = halves(gates)
    packet = jnp.concatenate([routed_in, gates_hi, gates_lo, jnp.zeros((rows, pad), BF16)], axis=1)

    turns = [0, 1]
    for i in range(2, deep // 2 + 1):
        turns += [deep + 1 - i, i]
    turns = turns[:deep]
    across = [("x", "y"), ("y", "x")]
    arrived = {0: packet}
    hops = {}
    ready = packet
    for at, turn in enumerate(turns):
        if turn:
            arrived[turn] = send(ready, z=-turn)
            if at == 2:
                ready = tie(packet, arrived[turns[1]])
    sums = {}
    gone = ()
    for at in range(0, deep, 2):
        pair = turns[at : at + 2]
        for turn in pair:
            hops[turn] = {"x": send(arrived[turn], x=1), "y": send(arrived[turn], y=1)}
        far = [
            send(tie(hops[turn][first], *gone) if gone else hops[turn][first], **{second: 1})
            for turn, (first, second) in zip(pair, across)
        ]
        shards = [arrived[t] for t in pair] + [hops[t]["x"] for t in pair] + [hops[t]["y"] for t in pair] + far
        done = run_experts(shards, chosen, weights, other, width, capacity)
        gone = (done[0],)
        for i, turn in enumerate(pair):
            sums[turn] = (done[i], {"x": done[2 + i], "y": done[4 + i]}, done[6 + i], across[i])
    total = []
    late = ()
    for turn in turns[1:] + [0]:
        own, to, far, (first, second) = sums[turn]
        if turn == 0 and late:
            far = tie(far, *late)
        back = send(far, **{second: 1})
        late = (back,)
        to[first] = plus(to[first], back).astype(BF16)
        got = [send(to[second], **{second: 1}), send(to[first], **{first: 1})]
        part = plus(own, *got)
        total.append(send(part.astype(BF16), z=turn).astype(F32) if turn else part)
    return plus(*total)


def routed_by_exchange(routed_in, gates, named, weights, capacity):
    rows, width = routed_in.shape
    expert_gate, expert_up, expert_down = weights
    local_count, experts = expert_gate.shape[0], gates.shape[1]
    count = experts // local_count
    earlier = jnp.dot(jnp.tril(jnp.ones((rows, rows), BF16), -1), named.astype(BF16), preferred_element_type=F32)
    slot = jnp.where(named, earlier.astype(jnp.int32), capacity)
    picks = (slot.T[:, None, :] == jnp.arange(capacity, dtype=jnp.int32)[None, :, None]).reshape(experts * capacity, rows)
    outgoing = jnp.dot(picks.astype(BF16), routed_in, preferred_element_type=F32).astype(BF16)
    received = lax.all_to_all(
        outgoing.reshape(count, local_count, capacity, width), AXES, split_axis=0, concat_axis=0, tiled=True
    )
    received = received.transpose(1, 0, 2, 3).reshape(local_count, count * capacity, width)
    gate_part = jnp.einsum("esd,edf->esf", received, expert_gate, preferred_element_type=F32)
    up_part = jnp.einsum("esd,edf->esf", received, expert_up, preferred_element_type=F32)
    hidden = (jax.nn.silu(gate_part) * up_part).astype(BF16)
    result = jnp.einsum("esf,efd->esd", hidden, expert_down, preferred_element_type=F32).astype(BF16)
    result = result.reshape(local_count, count, capacity, width).transpose(1, 0, 2, 3)
    returned = lax.all_to_all(result, AXES, split_axis=0, concat_axis=0, tiled=True)
    spread = jnp.where(slot[:, :, None] == jnp.arange(capacity, dtype=jnp.int32), gates[:, :, None], 0.0)
    spread_hi, spread_lo = halves(spread.reshape(rows, experts * capacity))
    pulled = jnp.dot(
        jnp.concatenate([spread_hi, spread_lo], axis=0),
        returned.reshape(experts * capacity, width),
        preferred_element_type=F32,
    )
    return pulled[:rows] + pulled[rows:]


def local(
    layout,
    residual,
    mixed_qkv,
    output_gate,
    log_decay,
    write_strength,
    conv_weight,
    norm_gain,
    out_weight,
    post_gain,
    router_weight,
    expert_ids,
    expert_gate,
    expert_up,
    expert_down,
    shared_gate,
    shared_up,
    shared_down,
    shared_switch,
):
    rows, width = residual.shape
    head = norm_gain.shape[0]
    count = lax.axis_size(AXES)
    place = lax.axis_index(AXES)
    before = lax.ppermute(mixed_qkv[rows - 8 :], AXES, [(i, i + 1) for i in range(count - 1)])
    weights = (expert_gate, expert_up, expert_down)
    x, y, z, cores = layout[1]
    paired = (x, y, cores) == (2, 2, 2) and z % 2 == 0
    across_y, across_core = moves(layout, y=1), moves(layout, core=1)
    columns = lax.axis_size("exp")
    near = columns == 4 and all(i // columns == j // columns for i, j in across_y + across_core)
    if near:
        out_parts = [out_weight, lax.ppermute(out_weight, AXES, across_y)]
        out_parts += [lax.ppermute(w, AXES, across_core) for w in out_parts]
        twin, facing = (jnp.asarray([j for _, j in sorted(pairs)], jnp.int32) for pairs in (across_core, across_y))
        owners = [p % columns for p in (place, facing[place], twin[place], facing[twin[place]])]
    if paired:
        other = [lax.ppermute(w, AXES, across_core) for w in weights]
    block_map, read = delta_terms(mixed_qkv, before, conv_weight, log_decay, write_strength, head)
    state = starting_states(block_map, count, place)
    normed = emit(read, state, output_gate, norm_gain)
    if near:
        products = [jnp.dot(normed, w, preferred_element_type=F32) for w in out_parts]
        projected = jnp.concatenate(
            [sum(jnp.where(o == e, p, 0.0) for o, p in zip(owners, products)) for e in range(columns)], axis=1
        )
    else:
        projected = jnp.dot(normed, lax.all_gather(out_weight, "exp", axis=1, tiled=True), preferred_element_type=F32)
    after_mix = (residual.astype(F32) + projected).astype(BF16)
    after_wide = after_mix.astype(F32)
    routed_in = (
        after_wide * lax.rsqrt(jnp.mean(after_wide * after_wide, axis=-1, keepdims=True) + EPS) * post_gain
    ).astype(BF16)

    experts = expert_gate.shape[0] * count
    capacity = rows * expert_ids.shape[1] * 6 // (experts * 5)
    named = jnp.any(expert_ids[:, :, None] == jnp.arange(experts, dtype=jnp.int32), axis=1)
    logits = jnp.dot(routed_in, router_weight, preferred_element_type=F32)
    chosen = jnp.where(named, jnp.exp(jnp.where(named, logits, 0.0)), 0.0)
    gates = chosen / jnp.sum(chosen, axis=1, keepdims=True)
    if paired:
        routed = routed_by_gather(layout, place, routed_in, gates, weights, other, capacity)
    else:
        routed = routed_by_exchange(routed_in, gates, named, weights, capacity)
    shared_hidden = (
        jax.nn.silu(jnp.dot(routed_in, shared_gate, preferred_element_type=F32))
        * jnp.dot(routed_in, shared_up, preferred_element_type=F32)
    ).astype(BF16)
    switch = jax.nn.sigmoid(jnp.dot(routed_in, shared_switch, preferred_element_type=F32))
    shared_out = switch[:, None] * jnp.dot(shared_hidden, shared_down, preferred_element_type=F32)
    return (after_wide + routed + shared_out).astype(BF16)


def solution(mesh):
    rows = P(AXES, None)
    return jax.shard_map(
        functools.partial(local, places(mesh)),
        mesh=mesh,
        in_specs=(rows, rows, rows, rows, rows, P(), P(), P(None, "exp"), P(), P(), rows)
        + (P(AXES, None, None),) * 3
        + (P(),) * 4,
        out_specs=rows,
        check_vma=False,
    )
```

```python
import functools

import jax
import jax.numpy as jnp
from jax import lax
from jax.experimental import pallas as pl
from jax.experimental.pallas import tpu as pltpu
from jax.sharding import PartitionSpec as P

AXES = ("ctx", "exp")
EPS = 1e-06
F32, BF16 = jnp.float32, jnp.bfloat16


def dot(a, b, dims=((1,), (0,))):
    return lax.dot_general(a, b, (dims, ((), ())), preferred_element_type=F32)


def halves(x):
    hi = x.astype(BF16)
    return hi, (x - hi.astype(F32)).astype(BF16)


def dot_square(a, b):
    n = b.shape[1]
    ah, al = halves(a)
    bh, bl = halves(b)
    left = jnp.concatenate([ah, al], axis=1)
    right = jnp.concatenate(
        [jnp.concatenate([bh, bl], axis=1), jnp.concatenate([bh, jnp.zeros_like(bl)], axis=1)], axis=0
    )
    both = dot(left, right)
    return both[:, :n] + both[:, n:]


def dot_wide(a, b):
    ah, al = halves(a)
    bh, bl = halves(b)
    return dot(jnp.concatenate([ah, al], axis=1), jnp.concatenate([bh, bh], axis=0)) + dot(ah, bl)


def unit_lower_inverse(lower):
    n = lower[0].shape[0]
    row = lax.broadcasted_iota(jnp.int32, (n, n), 0)
    col = lax.broadcasted_iota(jnp.int32, (n, n), 1)
    eye = jnp.where(row == col, 1.0, 0.0)
    size = 1
    done = None
    while size < n:
        pair = (row // (2 * size) == col // (2 * size)) & (row // size != col // size)
        corner = [jnp.where(pair, m, 0.0) for m in lower]
        if size == 1:
            done = [eye - c for c in corner]
        else:
            half = [dot_square(d, c) for d, c in zip(done, corner)]
            done = [d - dot_square(h, d) for d, h in zip(done, half)]
        size *= 2
    return done


def delta_kernel(q_ref, k_ref, v_ref, qb_ref, kb_ref, vb_ref, qw_ref, kw_ref, vw_ref, cols_ref, rows_ref, map_ref, read_ref, *, head, per):
    rows = q_ref.shape[0]
    groups = q_ref.shape[1] // head

    def conv(x_ref, b_ref, w_ref):
        x = jnp.concatenate([b_ref[...].astype(F32), x_ref[...].astype(F32)], axis=0)
        w = w_ref[...]
        y = w[3:4] * x[8 : 8 + rows]
        for tap in range(3):
            y = y + w[tap : tap + 1] * x[5 + tap : 5 + tap + rows]
        return y / (1.0 + jnp.exp(-y))

    def unit(x):
        return x * lax.rsqrt(jnp.sum(x * x, axis=-1, keepdims=True) + EPS)

    q_all, k_all, v_all = conv(q_ref, qb_ref, qw_ref), conv(k_ref, kb_ref, kw_ref), conv(v_ref, vb_ref, vw_ref)
    row = lax.broadcasted_iota(jnp.int32, (rows, rows), 0)
    col = lax.broadcasted_iota(jnp.int32, (rows, rows), 1)
    lower, info = [], []
    for g in range(groups):
        q = unit(q_all[:, g * head : (g + 1) * head]) * head**-0.5
        k = unit(k_all[:, g * head : (g + 1) * head])
        kh, kl = halves(k)
        qh, ql = halves(q)
        top = jnp.concatenate([jnp.concatenate([kh, kl], axis=1), jnp.concatenate([qh, ql], axis=1)], axis=0)
        inner = dot(top, jnp.concatenate([kh, kh], axis=1), ((1,), (1,)))
        inner = inner + dot(jnp.concatenate([kh, qh], axis=0), kl, ((1,), (1,)))
        kk, qk = inner[:rows], inner[rows:]
        for i in range(per):
            j = g * per + i
            cum_col = cols_ref[j, :, 0:1]
            strength = cols_ref[j, :, 1:2]
            cum_row = rows_ref[j, 0:1, :]
            gap = cum_col - cum_row
            ratios = jnp.where(row >= col, jnp.exp(jnp.where(row >= col, gap, 0.0)), 0.0)
            lower.append(jnp.where(row > col, ratios * kk, 0.0) * strength)
            info.append((q, k, v_all[:, j * head : (j + 1) * head], cum_col, strength, qk * ratios))
    inverse = unit_lower_inverse(lower)
    for j, (q, k, v, cum, strength, scores) in enumerate(info):
        decay = jnp.exp(cum)
        right = jnp.concatenate([strength * decay * k, strength * v], axis=1)
        solved = dot_wide(inverse[j], right)
        last = cum[rows - 1 : rows]
        to_end = k * jnp.exp(last - cum)
        update = dot_wide(to_end.T, solved)
        end = jnp.exp(last)
        diag = lax.broadcasted_iota(jnp.int32, (head, head), 0) == lax.broadcasted_iota(jnp.int32, (head, head), 1)
        map_ref[j, :, :head] = jnp.where(diag, end, 0.0) - update[:, :head]
        map_ref[j, :, head:] = update[:, head:]
        read = dot_wide(scores, solved)
        read_ref[j, :, :head] = q * decay - read[:, :head]
        read_ref[j, :, head:] = read[:, head:]


def delta_terms(mixed, before, conv_weight, log_decay, write_strength, head):
    rows, vheads = log_decay.shape
    kheads = (mixed.shape[1] // head - vheads) // 2
    per = vheads // kheads
    together = 2 if kheads % 2 == 0 else 1
    steps = kheads // together
    causal = jnp.tril(jnp.ones((rows, rows), F32))
    cumul = jnp.dot(causal, log_decay, precision=lax.Precision.HIGHEST)
    cols = jnp.stack([cumul.T, write_strength.T], axis=2)
    lines = cumul.T[:, None, :]
    qw, vw = together * head, together * per * head
    k_at, v_at = kheads * head // qw, 2 * kheads * head // vw

    def spec(height, width, at):
        return pl.BlockSpec((height, width), lambda s: (0, s + at))

    n = together * per
    return pl.pallas_call(
        functools.partial(delta_kernel, head=head, per=per),
        grid=(steps,),
        in_specs=[spec(h, w, a) for h in (rows, 8, 4) for w, a in ((qw, 0), (qw, k_at), (vw, v_at))]
        + [
            pl.BlockSpec((n, rows, 2), lambda s: (s, 0, 0)),
            pl.BlockSpec((n, 1, rows), lambda s: (s, 0, 0)),
        ],
        out_specs=[pl.BlockSpec((n, head, 2 * head), lambda s: (s, 0, 0)), pl.BlockSpec((n, rows, 2 * head), lambda s: (s, 0, 0))],
        out_shape=[jax.ShapeDtypeStruct((vheads, head, 2 * head), F32), jax.ShapeDtypeStruct((vheads, rows, 2 * head), F32)],
        cost_estimate=pl.CostEstimate(flops=rows * head * head * vheads, bytes_accessed=rows * head * vheads, transcendentals=0),
        compiler_params=pltpu.CompilerParams(vmem_limit_bytes=40 * 2**20),
        name="delta_terms",
    )(mixed, mixed, mixed, before, before, before, conv_weight, conv_weight, conv_weight, cols, lines)


def emit_kernel(read_ref, state_ref, gate_ref, gain_ref, out_ref):
    n, rows, head2 = read_ref.shape
    head = head2 // 2
    for j in range(n):
        out = dot_square(read_ref[j, :, :head], state_ref[j]) + read_ref[j, :, head:]
        normed = out * lax.rsqrt(jnp.mean(out * out, axis=-1, keepdims=True) + EPS)
        gate = gate_ref[:, j * head : (j + 1) * head].astype(F32)
        out_ref[:, j * head : (j + 1) * head] = (normed * gain_ref[...] * (gate / (1.0 + jnp.exp(-gate)))).astype(BF16)


def emit(read, state, output_gate, gain):
    vheads, rows, head2 = read.shape
    head = head2 // 2
    n = 4 if vheads % 4 == 0 else 1
    return pl.pallas_call(
        emit_kernel,
        grid=(vheads // n,),
        in_specs=[
            pl.BlockSpec((n, rows, head2), lambda s: (s, 0, 0)),
            pl.BlockSpec((n, head, head), lambda s: (s, 0, 0)),
            pl.BlockSpec((rows, n * head), lambda s: (0, s)),
            pl.BlockSpec((1, head), lambda s: (0, 0)),
        ],
        out_specs=pl.BlockSpec((rows, n * head), lambda s: (0, s)),
        out_shape=jax.ShapeDtypeStruct((rows, vheads * head), BF16),
        name="emit",
    )(read, state, output_gate, gain[None])


def tie(value, *after):
    return lax.optimization_barrier((value, *after))[0]


def apply(transform, right):
    return jnp.einsum("hij,hjk->hik", transform, right, precision=lax.Precision.HIGHEST)


def starting_states(block_map, count, place, first_half):
    head = block_map.shape[1]
    levels, step = [], 1
    held, some = block_map, None
    while count % (2 * step) == 0 and 4 * step < count and held.shape[0] % 2 == 0:
        share = held.shape[0] // 2
        upper = (place // step) % 2 == 1
        keep = jnp.where(upper, held[share:], held[:share])
        give = jnp.where(upper, held[:share], held[share:])
        kind = F32 if step == 1 else BF16
        got = lax.ppermute(give.astype(kind), AXES, [(i, i ^ step) for i in range(count)]).astype(F32)
        if step == 2 and first_half is not None:
            some = first_half(got)
        early, late = jnp.where(upper, got, keep), jnp.where(upper, keep, got)
        merged = apply(late[:, :, :head], early)
        held = jnp.concatenate([merged[:, :, :head], merged[:, :, head:] + late[:, :, head:]], axis=2)
        levels.append((step, upper, early))
        step *= 2
    state = jnp.zeros_like(held[:, :, head:])
    for turn in range(count // step - 1):
        ahead = held[:, :, head:]
        if turn:
            ahead = ahead + apply(held[:, :, :head], state)
        state = lax.ppermute(ahead.astype(BF16), AXES, [(i, i + step) for i in range(count - step)]).astype(F32)
    middle = state
    for step, upper, early in reversed(levels):
        second = apply(early[:, :, :head], state) + early[:, :, head:]
        mine, other = jnp.where(upper, second, state), jnp.where(upper, state, second)
        got = lax.ppermute(other.astype(BF16), AXES, [(i, i ^ step) for i in range(count)]).astype(F32)
        state = jnp.where(upper, jnp.concatenate([got, mine], axis=0), jnp.concatenate([mine, got], axis=0))
    return state, some, middle


def places(mesh):
    at = {(*d.coords, d.core_on_chip): i for i, d in enumerate(mesh.devices.flat)}
    return at, tuple(max(c[k] for c in at) + 1 for k in range(4))


def moves_to(layout, target):
    at, _ = layout
    return [(i, at[target(spot)]) for spot, i in at.items()]


def moves(layout, x=0, y=0, z=0, core=0):
    at, size = layout
    shift = (x, y, z, core)
    return [(i, at[tuple((c + s) % n for c, s, n in zip(spot, shift, size))]) for spot, i in at.items()]


def flip(layout, **by):
    masks = {i ^ j for i, j in moves(layout, **by)}
    return masks.pop() if len(masks) == 1 else None


def expert_kernel(*refs, width, capacity, local_count):
    shards, (chosen_ref, *weights), outs = refs[:8], refs[8:15], refs[15:23]
    block_ref, gate_w, up_w, down_w, sel_ref, pick_ref, gate_ref, back_ref, out_ref, in_sem, w_sem, out_sem = refs[23:]
    steps = 2 * local_count
    rows = shards[0].shape[0]
    pair_rows, slots = 2 * rows, 2 * capacity
    tile = width // 4
    packet = shards[0].shape[1]

    loads = [pltpu.make_async_copy(r, block_ref.at[i], in_sem.at[i]) for i, r in enumerate(shards)]
    fills = []
    for e in range(steps):
        part = weights[:3] if e < local_count else weights[3:]
        fills.append(
            [
                pltpu.make_async_copy(r.at[e % local_count], w.at[e], w_sem.at[e, k])
                for k, (r, w) in enumerate(zip(part, (gate_w, up_w, down_w)))
            ]
        )
    for copy in loads + sum(fills, []):
        copy.start()

    before = lax.broadcasted_iota(jnp.int32, (pair_rows, pair_rows), 0)
    after = lax.broadcasted_iota(jnp.int32, (pair_rows, pair_rows), 1)
    earlier = jnp.where((before < after) & (before // rows == after // rows), 1.0, 0.0).astype(BF16)
    second = lax.broadcasted_iota(jnp.int32, (1, pair_rows), 1) // rows
    slot = lax.broadcasted_iota(jnp.int32, (slots, pair_rows), 0)
    for p in range(4):
        loads[2 * p].wait()
        loads[2 * p + 1].wait()
        marks = block_ref[2 * p : 2 * p + 2, :, width:].reshape(pair_rows, packet - width)
        gates = dot(chosen_ref[...], marks, ((1,), (1,)))
        named = jnp.where(gates != 0.0, 1.0, 0.0)
        rank = dot(named.astype(BF16), earlier).astype(jnp.int32)
        spot = jnp.where(gates != 0.0, rank + second * capacity, -1)
        for e in range(steps):
            hit = slot == spot[e : e + 1]
            pick_ref[p, e * slots : (e + 1) * slots, :] = jnp.where(hit, 1.0, 0.0).astype(BF16)
            gate = jnp.sum(jnp.where(hit, gates[e : e + 1], 0.0), axis=1, keepdims=True)
            gate_ref[e, p * slots : (p + 1) * slots, :] = jnp.broadcast_to(gate, (slots, 128))
        for n in range(4):
            cut = slice(n * tile, (n + 1) * tile)
            taken = dot(pick_ref[p], block_ref[2 * p : 2 * p + 2, :, cut].reshape(pair_rows, tile)).astype(BF16)
            for e in range(steps):
                sel_ref[e, p * slots : (p + 1) * slots, cut] = taken[e * slots : (e + 1) * slots]

    for e in range(steps):
        for copy in fills[e]:
            copy.wait()
        rows_in = sel_ref[e]
        gate, up = dot(rows_in, gate_w[e]), dot(rows_in, up_w[e])
        hidden = (gate / (1.0 + jnp.exp(-gate)) * up).astype(BF16)
        weight = gate_ref[e][:, 0:1]
        for n in range(4):
            cut = slice(n * tile, (n + 1) * tile)
            result = (dot(hidden, down_w[e, :, cut]) * weight).astype(BF16)
            for p in range(4):
                back_ref[p, e * slots : (e + 1) * slots, cut] = result[p * slots : (p + 1) * slots]

    stores = [pltpu.make_async_copy(out_ref.at[i], r, out_sem.at[i]) for i, r in enumerate(outs)]
    for p in range(4):
        spread = pick_ref[p].astype(F32).T.astype(BF16)
        for n in range(4):
            cut = slice(n * tile, (n + 1) * tile)
            total = dot(spread, back_ref[p, :, cut]).astype(BF16)
            out_ref[2 * p : 2 * p + 2, :, cut] = total.reshape(2, rows, tile)
        stores[2 * p].start()
        stores[2 * p + 1].start()
    for copy in stores:
        copy.wait()


def run_experts(shards, chosen, mine, other, width, capacity):
    local_count, _, hidden = mine[0].shape
    steps = 2 * local_count
    slots = 2 * capacity
    rows, packet = shards[0].shape
    anywhere = pl.BlockSpec(memory_space=pl.ANY)
    return pl.pallas_call(
        functools.partial(expert_kernel, width=width, capacity=capacity, local_count=local_count),
        in_specs=[anywhere] * 8 + [pl.BlockSpec(memory_space=pltpu.VMEM)] + [anywhere] * 6,
        out_specs=[anywhere] * 8,
        out_shape=[jax.ShapeDtypeStruct((rows, width), BF16)] * 8,
        scratch_shapes=[
            pltpu.VMEM((8, rows, packet), BF16),
            pltpu.VMEM((steps, width, hidden), BF16),
            pltpu.VMEM((steps, width, hidden), BF16),
            pltpu.VMEM((steps, hidden, width), BF16),
            pltpu.VMEM((steps, 4 * slots, width), BF16),
            pltpu.VMEM((4, steps * slots, 2 * rows), BF16),
            pltpu.VMEM((steps, 4 * slots, 128), F32),
            pltpu.VMEM((4, steps * slots, width), BF16),
            pltpu.VMEM((8, rows, width), BF16),
            pltpu.SemaphoreType.DMA((8,)),
            pltpu.SemaphoreType.DMA((steps, 3)),
            pltpu.SemaphoreType.DMA((8,)),
        ],
        cost_estimate=pl.CostEstimate(
            flops=steps * 4 * slots * (6 * width * hidden + 8 * width * rows),
            bytes_accessed=6 * width * hidden * steps + 32 * rows * width,
            transcendentals=0,
        ),
        compiler_params=pltpu.CompilerParams(vmem_limit_bytes=56 * 2**20),
        name="experts",
    )(*shards, chosen, *mine, *other)


def plus(*parts):
    return sum(p.astype(F32) for p in parts[1:]) + parts[0].astype(F32)


class Links:
    def __init__(self, layout):
        self.layout, self.sent = layout, {}

    def send(self, value, link, turn=1):
        queue = self.sent.setdefault(link, [])
        if len(queue) >= 2:
            value = tie(value, queue[-2])
        queue.append(lax.ppermute(value, AXES, moves(self.layout, **{link: turn})))
        return queue[-1]


def routed_by_gather(layout, place, twin, routed_in, gates, weights, other, capacity):
    rows, width = routed_in.shape
    experts = gates.shape[1]
    local_count = weights[0].shape[0]
    deep = layout[1][2]
    ids = jnp.concatenate([p * local_count + jnp.arange(local_count, dtype=jnp.int32) for p in (place, place ^ twin)])
    ids = jnp.pad(ids, (0, -ids.shape[0] % 8), constant_values=experts)
    chosen = (ids[:, None] == jnp.arange(experts, dtype=jnp.int32)).astype(BF16)
    pad = -(2 * experts) % 128
    chosen = jnp.pad(jnp.concatenate([chosen, chosen], axis=1), ((0, 0), (0, pad)))
    gates_hi, gates_lo = halves(gates)
    packet = jnp.concatenate([routed_in, gates_hi, gates_lo, jnp.zeros((rows, pad), BF16)], axis=1)
    packet = tie(packet, *other)

    links = Links(layout)
    here = {0: packet}
    by_x, by_y, far, sums = {}, {}, {}, {}
    pairs = [(t, t + 1) for t in range(0, deep, 2)]

    def spread(t):
        by_x[t], by_y[t] = links.send(here[t], "x"), links.send(here[t], "y")
        if t + 1 < deep:
            here[t + 1] = links.send(here[t], "z", -1)

    for a, b in pairs:
        if a == 0:
            spread(a)
            spread(b)
        far[a], far[b] = links.send(by_x[a], "y"), links.send(by_y[b], "x")
        ahead = [sums[a - 1][0]] if a else []
        if b + 1 < deep:
            spread(b + 1)
            spread(b + 2)
            ahead += [by_x[b + 2], by_y[b + 2]]
        shards = [d[t] for d in (here, by_x, by_y, far) for t in (a, b)]
        done = run_experts([tie(shards[0], *ahead), *shards[1:]], chosen, weights, other, width, capacity)
        sums[a], sums[b] = done[0::2], done[1::2]
    links = Links(layout)

    def own_turn(t, straight, with_far):
        part = plus(sums[t][0], straight, with_far)
        return lax.ppermute(part.astype(BF16), AXES, moves(layout, z=t)) if t else part

    def added(block, back):
        return plus(block, back).astype(BF16)

    back1 = links.send(sums[1][3], "x")
    back0 = links.send(sums[0][3], "y")
    straight1 = links.send(sums[1][1], "x")
    last1 = links.send(added(sums[1][2], back1), "y")
    total = [own_turn(1, straight1, last1)]
    for a, b in pairs[1:]:
        back_b, back_a = links.send(sums[b][3], "x"), links.send(sums[a][3], "y")
        last_a, straight_a = links.send(added(sums[a][1], back_a), "x"), links.send(sums[a][2], "y")
        total.append(own_turn(a, straight_a, last_a))
        straight_b, last_b = links.send(sums[b][1], "x"), links.send(added(sums[b][2], back_b), "y")
        total.append(own_turn(b, straight_b, last_b))
    last0 = links.send(added(tie(sums[0][1], total[0]), back0), "x")
    straight0 = links.send(tie(sums[0][2], total[0]), "y")
    return plus(own_turn(0, straight0, last0), *total)


def routed_by_exchange(routed_in, gates, named, weights, capacity):
    rows, width = routed_in.shape
    expert_gate, expert_up, expert_down = weights
    local_count, experts = expert_gate.shape[0], gates.shape[1]
    count = experts // local_count
    earlier = jnp.dot(jnp.tril(jnp.ones((rows, rows), BF16), -1), named.astype(BF16), preferred_element_type=F32)
    slot = jnp.where(named, earlier.astype(jnp.int32), capacity)
    picks = (slot.T[:, None, :] == jnp.arange(capacity, dtype=jnp.int32)[None, :, None]).reshape(experts * capacity, rows)
    outgoing = jnp.dot(picks.astype(BF16), routed_in, preferred_element_type=F32).astype(BF16)
    received = lax.all_to_all(
        outgoing.reshape(count, local_count, capacity, width), AXES, split_axis=0, concat_axis=0, tiled=True
    )
    received = received.transpose(1, 0, 2, 3).reshape(local_count, count * capacity, width)
    gate_part = jnp.einsum("esd,edf->esf", received, expert_gate, preferred_element_type=F32)
    up_part = jnp.einsum("esd,edf->esf", received, expert_up, preferred_element_type=F32)
    hidden = (jax.nn.silu(gate_part) * up_part).astype(BF16)
    result = jnp.einsum("esf,efd->esd", hidden, expert_down, preferred_element_type=F32).astype(BF16)
    result = result.reshape(local_count, count, capacity, width).transpose(1, 0, 2, 3)
    returned = lax.all_to_all(result, AXES, split_axis=0, concat_axis=0, tiled=True)
    spread = jnp.where(slot[:, :, None] == jnp.arange(capacity, dtype=jnp.int32), gates[:, :, None], 0.0)
    spread_hi, spread_lo = halves(spread.reshape(rows, experts * capacity))
    pulled = jnp.dot(
        jnp.concatenate([spread_hi, spread_lo], axis=0),
        returned.reshape(experts * capacity, width),
        preferred_element_type=F32,
    )
    return pulled[:rows] + pulled[rows:]


def local(
    layout,
    residual,
    mixed_qkv,
    output_gate,
    log_decay,
    write_strength,
    conv_weight,
    norm_gain,
    out_weight,
    post_gain,
    router_weight,
    expert_ids,
    expert_gate,
    expert_up,
    expert_down,
    shared_gate,
    shared_up,
    shared_down,
    shared_switch,
):
    rows, width = residual.shape
    head = norm_gain.shape[0]
    count = lax.axis_size(AXES)
    place = lax.axis_index(AXES)
    before = lax.ppermute(mixed_qkv[rows - 8 :], AXES, [(i, i + 1) for i in range(count - 1)])
    weights = (expert_gate, expert_up, expert_down)
    x, y, z, cores = layout[1]
    twin, facing = flip(layout, core=1), flip(layout, y=1)
    paired = (x, y, cores) == (2, 2, 2) and z % 2 == 0 and twin is not None
    columns = lax.axis_size("exp")
    beside = {i ^ j for i, j in moves_to(layout, lambda c: (c[0], c[1], c[2] ^ 1, c[3]))} if z % 2 == 0 else set()
    near = columns == 4 and None not in (twin, facing) and twin | facing == columns - 1 and len(beside) == 1
    if paired:
        other = [lax.ppermute(w, AXES, moves(layout, core=1)) for w in weights]
    block_map, read = delta_terms(mixed_qkv, before, conv_weight, log_decay, write_strength, head)
    half = out_weight.shape[0] // 2
    odd = (place & min(beside)) != 0 if near else None

    def first_half(done):
        mine = tie(jnp.where(odd, out_weight[half:], out_weight[:half]), done)
        return lax.ppermute(mine, AXES, moves(layout, y=1))

    state, some, middle = starting_states(block_map, count, place, first_half if near else None)
    if near:
        rest = lax.ppermute(tie(some, middle), AXES, moves_to(layout, lambda c: (c[0], c[1], c[2] ^ 1, c[3])))
        out_parts = [[out_weight], [some, rest]]
        out_parts += [[lax.ppermute(w, AXES, moves(layout, core=1)) for w in part] for part in out_parts]
        owners = [(place ^ mask) % columns for mask in (0, facing, twin, facing | twin)]
    normed = emit(read, state, output_gate, norm_gain)
    if near:
        mine = jnp.where(odd, normed[:, half:], normed[:, :half])
        others = jnp.where(odd, normed[:, :half], normed[:, half:])
        products = []
        for part in out_parts:
            by = [normed] if len(part) == 1 else [mine, others]
            products.append(sum(jnp.dot(n, w, preferred_element_type=F32) for n, w in zip(by, part)))
        projected = jnp.concatenate(
            [sum(jnp.where(o == e, p, 0.0) for o, p in zip(owners, products)) for e in range(columns)], axis=1
        )
    else:
        projected = jnp.dot(normed, lax.all_gather(out_weight, "exp", axis=1, tiled=True), preferred_element_type=F32)
    after_mix = (residual.astype(F32) + projected).astype(BF16)
    after_wide = after_mix.astype(F32)
    routed_in = (
        after_wide * lax.rsqrt(jnp.mean(after_wide * after_wide, axis=-1, keepdims=True) + EPS) * post_gain
    ).astype(BF16)

    experts = expert_gate.shape[0] * count
    capacity = rows * expert_ids.shape[1] * 6 // (experts * 5)
    named = jnp.any(expert_ids[:, :, None] == jnp.arange(experts, dtype=jnp.int32), axis=1)
    logits = jnp.dot(routed_in, router_weight, preferred_element_type=F32)
    chosen = jnp.where(named, jnp.exp(jnp.where(named, logits, 0.0)), 0.0)
    gates = chosen / jnp.sum(chosen, axis=1, keepdims=True)
    if paired:
        routed = routed_by_gather(layout, place, twin, routed_in, gates, weights, other, capacity)
    else:
        routed = routed_by_exchange(routed_in, gates, named, weights, capacity)
    shared_hidden = (
        jax.nn.silu(jnp.dot(routed_in, shared_gate, preferred_element_type=F32))
        * jnp.dot(routed_in, shared_up, preferred_element_type=F32)
    ).astype(BF16)
    switch = jax.nn.sigmoid(jnp.dot(routed_in, shared_switch, preferred_element_type=F32))
    shared_out = switch[:, None] * jnp.dot(shared_hidden, shared_down, preferred_element_type=F32)
    return (after_wide + routed + shared_out).astype(BF16)


def solution(mesh):
    rows = P(AXES, None)
    return jax.shard_map(
        functools.partial(local, places(mesh)),
        mesh=mesh,
        in_specs=(rows, rows, rows, rows, rows, P(), P(), P(None, "exp"), P(), P(), rows)
        + (P(AXES, None, None),) * 3
        + (P(),) * 4,
        out_specs=rows,
        check_vma=False,
    )
```

```python
import functools

import jax
import jax.numpy as jnp
from jax import lax
from jax.experimental import pallas as pl
from jax.experimental.pallas import tpu as pltpu
from jax.sharding import PartitionSpec as P

AXES = ("ctx", "exp")
EPS = 1e-06
F32, BF16 = jnp.float32, jnp.bfloat16


def dot(a, b, dims=((1,), (0,))):
    return lax.dot_general(a, b, (dims, ((), ())), preferred_element_type=F32)


def halves(x):
    hi = x.astype(BF16)
    return hi, (x - hi.astype(F32)).astype(BF16)


def dot_square(a, b):
    n = b.shape[1]
    ah, al = halves(a)
    bh, bl = halves(b)
    left = jnp.concatenate([ah, al], axis=1)
    right = jnp.concatenate(
        [jnp.concatenate([bh, bl], axis=1), jnp.concatenate([bh, jnp.zeros_like(bl)], axis=1)], axis=0
    )
    both = dot(left, right)
    return both[:, :n] + both[:, n:]


def dot_wide(a, b):
    ah, al = halves(a)
    bh, bl = halves(b)
    return dot(jnp.concatenate([ah, al], axis=1), jnp.concatenate([bh, bh], axis=0)) + dot(ah, bl)


def unit_lower_inverse(lower):
    n = lower[0].shape[0]
    row = lax.broadcasted_iota(jnp.int32, (n, n), 0)
    col = lax.broadcasted_iota(jnp.int32, (n, n), 1)
    eye = jnp.where(row == col, 1.0, 0.0)
    size = 1
    done = None
    while size < n:
        pair = (row // (2 * size) == col // (2 * size)) & (row // size != col // size)
        corner = [jnp.where(pair, m, 0.0) for m in lower]
        if size == 1:
            done = [eye - c for c in corner]
        else:
            half = [dot_square(d, c) for d, c in zip(done, corner)]
            done = [d - dot_square(h, d) for d, h in zip(done, half)]
        size *= 2
    return done


def delta_kernel(q_ref, k_ref, v_ref, qb_ref, kb_ref, vb_ref, qw_ref, kw_ref, vw_ref, cols_ref, rows_ref, map_ref, read_ref, *, head, per):
    rows = q_ref.shape[0]
    groups = q_ref.shape[1] // head

    def conv(x_ref, b_ref, w_ref):
        x = jnp.concatenate([b_ref[...].astype(F32), x_ref[...].astype(F32)], axis=0)
        w = w_ref[...]
        y = w[3:4] * x[8 : 8 + rows]
        for tap in range(3):
            y = y + w[tap : tap + 1] * x[5 + tap : 5 + tap + rows]
        return y / (1.0 + jnp.exp(-y))

    def unit(x):
        return x * lax.rsqrt(jnp.sum(x * x, axis=-1, keepdims=True) + EPS)

    q_all, k_all, v_all = conv(q_ref, qb_ref, qw_ref), conv(k_ref, kb_ref, kw_ref), conv(v_ref, vb_ref, vw_ref)
    row = lax.broadcasted_iota(jnp.int32, (rows, rows), 0)
    col = lax.broadcasted_iota(jnp.int32, (rows, rows), 1)
    lower, info = [], []
    for g in range(groups):
        q = unit(q_all[:, g * head : (g + 1) * head]) * head**-0.5
        k = unit(k_all[:, g * head : (g + 1) * head])
        kh, kl = halves(k)
        qh, ql = halves(q)
        top = jnp.concatenate([jnp.concatenate([kh, kl], axis=1), jnp.concatenate([qh, ql], axis=1)], axis=0)
        inner = dot(top, jnp.concatenate([kh, kh], axis=1), ((1,), (1,)))
        inner = inner + dot(jnp.concatenate([kh, qh], axis=0), kl, ((1,), (1,)))
        kk, qk = inner[:rows], inner[rows:]
        for i in range(per):
            j = g * per + i
            cum_col = cols_ref[j, :, 0:1]
            strength = cols_ref[j, :, 1:2]
            cum_row = rows_ref[j, 0:1, :]
            gap = cum_col - cum_row
            ratios = jnp.where(row >= col, jnp.exp(jnp.where(row >= col, gap, 0.0)), 0.0)
            lower.append(jnp.where(row > col, ratios * kk, 0.0) * strength)
            info.append((q, k, v_all[:, j * head : (j + 1) * head], cum_col, strength, qk * ratios))
    inverse = unit_lower_inverse(lower)
    for j, (q, k, v, cum, strength, scores) in enumerate(info):
        decay = jnp.exp(cum)
        right = jnp.concatenate([strength * decay * k, strength * v], axis=1)
        solved = dot_wide(inverse[j], right)
        last = cum[rows - 1 : rows]
        to_end = k * jnp.exp(last - cum)
        update = dot_wide(to_end.T, solved)
        end = jnp.exp(last)
        diag = lax.broadcasted_iota(jnp.int32, (head, head), 0) == lax.broadcasted_iota(jnp.int32, (head, head), 1)
        map_ref[j, :, :head] = jnp.where(diag, end, 0.0) - update[:, :head]
        map_ref[j, :, head:] = update[:, head:]
        read = dot_wide(scores, solved)
        read_ref[j, :, :head] = q * decay - read[:, :head]
        read_ref[j, :, head:] = read[:, head:]


def delta_terms(mixed, before, conv_weight, log_decay, write_strength, head):
    rows, vheads = log_decay.shape
    kheads = (mixed.shape[1] // head - vheads) // 2
    per = vheads // kheads
    together = 2 if kheads % 2 == 0 else 1
    steps = kheads // together
    causal = jnp.tril(jnp.ones((rows, rows), F32))
    cumul = jnp.dot(causal, log_decay, precision=lax.Precision.HIGHEST)
    cols = jnp.stack([cumul.T, write_strength.T], axis=2)
    lines = cumul.T[:, None, :]
    qw, vw = together * head, together * per * head
    k_at, v_at = kheads * head // qw, 2 * kheads * head // vw

    def spec(height, width, at):
        return pl.BlockSpec((height, width), lambda s: (0, s + at))

    n = together * per
    return pl.pallas_call(
        functools.partial(delta_kernel, head=head, per=per),
        grid=(steps,),
        in_specs=[spec(h, w, a) for h in (rows, 8, 4) for w, a in ((qw, 0), (qw, k_at), (vw, v_at))]
        + [
            pl.BlockSpec((n, rows, 2), lambda s: (s, 0, 0)),
            pl.BlockSpec((n, 1, rows), lambda s: (s, 0, 0)),
        ],
        out_specs=[pl.BlockSpec((n, head, 2 * head), lambda s: (s, 0, 0)), pl.BlockSpec((n, rows, 2 * head), lambda s: (s, 0, 0))],
        out_shape=[jax.ShapeDtypeStruct((vheads, head, 2 * head), F32), jax.ShapeDtypeStruct((vheads, rows, 2 * head), F32)],
        cost_estimate=pl.CostEstimate(flops=rows * head * head * vheads, bytes_accessed=rows * head * vheads, transcendentals=0),
        compiler_params=pltpu.CompilerParams(vmem_limit_bytes=40 * 2**20),
        name="delta_terms",
    )(mixed, mixed, mixed, before, before, before, conv_weight, conv_weight, conv_weight, cols, lines)


def emit_kernel(read_ref, state_ref, gate_ref, gain_ref, out_ref):
    n, rows, head2 = read_ref.shape
    head = head2 // 2
    for j in range(n):
        out = dot_square(read_ref[j, :, :head], state_ref[j]) + read_ref[j, :, head:]
        normed = out * lax.rsqrt(jnp.mean(out * out, axis=-1, keepdims=True) + EPS)
        gate = gate_ref[:, j * head : (j + 1) * head].astype(F32)
        out_ref[:, j * head : (j + 1) * head] = (normed * gain_ref[...] * (gate / (1.0 + jnp.exp(-gate)))).astype(BF16)


def emit(read, state, output_gate, gain):
    vheads, rows, head2 = read.shape
    head = head2 // 2
    n = 4 if vheads % 4 == 0 else 1
    return pl.pallas_call(
        emit_kernel,
        grid=(vheads // n,),
        in_specs=[
            pl.BlockSpec((n, rows, head2), lambda s: (s, 0, 0)),
            pl.BlockSpec((n, head, head), lambda s: (s, 0, 0)),
            pl.BlockSpec((rows, n * head), lambda s: (0, s)),
            pl.BlockSpec((1, head), lambda s: (0, 0)),
        ],
        out_specs=pl.BlockSpec((rows, n * head), lambda s: (0, s)),
        out_shape=jax.ShapeDtypeStruct((rows, vheads * head), BF16),
        name="emit",
    )(read, state, output_gate, gain[None])


def tie(value, *after):
    return lax.optimization_barrier((value, *after))[0]


def apply(transform, right):
    return jnp.einsum("hij,hjk->hik", transform, right, precision=lax.Precision.HIGHEST)


def starting_states(block_map, count, place, ready, swaps):
    head = block_map.shape[1]
    levels, step = [], 1
    held = block_map
    while count % (2 * step) == 0 and 4 * step < count and held.shape[0] % 2 == 0:
        share = held.shape[0] // 2
        upper = (place // step) % 2 == 1
        keep = jnp.where(upper, held[share:], held[:share])
        give = jnp.where(upper, held[:share], held[share:])
        kind = F32 if step == 1 else BF16
        if step == 1 and ready is not None:
            give = tie(give, ready)
        got = lax.ppermute(give.astype(kind), AXES, [(i, i ^ step) for i in range(count)]).astype(F32)
        early, late = jnp.where(upper, got, keep), jnp.where(upper, keep, got)
        merged = apply(late[:, :, :head], early)
        held = jnp.concatenate([merged[:, :, :head], merged[:, :, head:] + late[:, :, head:]], axis=2)
        levels.append((step, upper, early))
        step *= 2
    state = jnp.zeros_like(held[:, :, head:])
    for turn in range(count // step - 1):
        ahead = held[:, :, head:]
        if turn:
            ahead = ahead + apply(held[:, :, :head], state)
        state = lax.ppermute(ahead.astype(BF16), AXES, [(i, i + step) for i in range(count - step)]).astype(F32)
    middle = state
    state = tie(state, *swaps)
    for step, upper, early in reversed(levels):
        second = apply(early[:, :, :head], state) + early[:, :, head:]
        mine, other = jnp.where(upper, second, state), jnp.where(upper, state, second)
        got = lax.ppermute(other.astype(BF16), AXES, [(i, i ^ step) for i in range(count)]).astype(F32)
        state = jnp.where(upper, jnp.concatenate([got, mine], axis=0), jnp.concatenate([mine, got], axis=0))
    return state, middle


def places(mesh):
    at = {(*d.coords, d.core_on_chip): i for i, d in enumerate(mesh.devices.flat)}
    return at, tuple(max(c[k] for c in at) + 1 for k in range(4))


def moves_to(layout, target):
    at, _ = layout
    return [(i, at[target(spot)]) for spot, i in at.items()]


def moves(layout, x=0, y=0, z=0, core=0):
    at, size = layout
    shift = (x, y, z, core)
    return [(i, at[tuple((c + s) % n for c, s, n in zip(spot, shift, size))]) for spot, i in at.items()]


def flip(layout, **by):
    masks = {i ^ j for i, j in moves(layout, **by)}
    return masks.pop() if len(masks) == 1 else None


def expert_kernel(*refs, width, capacity, local_count):
    shards, (chosen_ref, *weights), outs = refs[:8], refs[8:15], refs[15:23]
    block_ref, gate_w, up_w, down_w, sel_ref, pick_ref, gate_ref, back_ref, out_ref, in_sem, w_sem, out_sem = refs[23:]
    steps = 2 * local_count
    rows = shards[0].shape[0]
    pair_rows, slots = 2 * rows, 2 * capacity
    tile = width // 4
    packet = shards[0].shape[1]

    loads = [pltpu.make_async_copy(r, block_ref.at[i], in_sem.at[i]) for i, r in enumerate(shards)]
    fills = []
    for e in range(steps):
        part = weights[:3] if e < local_count else weights[3:]
        fills.append(
            [
                pltpu.make_async_copy(r.at[e % local_count], w.at[e % 2], w_sem.at[e, k])
                for k, (r, w) in enumerate(zip(part, (gate_w, up_w, down_w)))
            ]
        )
    for copy in loads + fills[0] + fills[1]:
        copy.start()

    before = lax.broadcasted_iota(jnp.int32, (pair_rows, pair_rows), 0)
    after = lax.broadcasted_iota(jnp.int32, (pair_rows, pair_rows), 1)
    earlier = jnp.where((before < after) & (before // rows == after // rows), 1.0, 0.0).astype(BF16)
    second = lax.broadcasted_iota(jnp.int32, (1, pair_rows), 1) // rows
    slot = lax.broadcasted_iota(jnp.int32, (slots, pair_rows), 0)
    for p in range(4):
        loads[2 * p].wait()
        loads[2 * p + 1].wait()
        marks = block_ref[2 * p : 2 * p + 2, :, width:].reshape(pair_rows, packet - width)
        gates = dot(chosen_ref[...], marks, ((1,), (1,)))
        named = jnp.where(gates != 0.0, 1.0, 0.0)
        rank = dot(named.astype(BF16), earlier).astype(jnp.int32)
        spot = jnp.where(gates != 0.0, rank + second * capacity, -1)
        for e in range(steps):
            hit = slot == spot[e : e + 1]
            pick_ref[p, e * slots : (e + 1) * slots, :] = jnp.where(hit, 1.0, 0.0).astype(BF16)
            gate = jnp.sum(jnp.where(hit, gates[e : e + 1], 0.0), axis=1, keepdims=True)
            gate_ref[e, p * slots : (p + 1) * slots, :] = jnp.broadcast_to(gate, (slots, 128))
        for n in range(4):
            cut = slice(n * tile, (n + 1) * tile)
            taken = dot(pick_ref[p], block_ref[2 * p : 2 * p + 2, :, cut].reshape(pair_rows, tile)).astype(BF16)
            for e in range(steps):
                sel_ref[e, p * slots : (p + 1) * slots, cut] = taken[e * slots : (e + 1) * slots]

    for e in range(steps):
        for copy in fills[e]:
            copy.wait()
        rows_in = sel_ref[e]
        gate, up = dot(rows_in, gate_w[e % 2]), dot(rows_in, up_w[e % 2])
        hidden = (gate / (1.0 + jnp.exp(-gate)) * up).astype(BF16)
        weight = gate_ref[e][:, 0:1]
        for n in range(4):
            cut = slice(n * tile, (n + 1) * tile)
            result = (dot(hidden, down_w[e % 2, :, cut]) * weight).astype(BF16)
            for p in range(4):
                back_ref[p, e * slots : (e + 1) * slots, cut] = result[p * slots : (p + 1) * slots]
        if e + 2 < steps:
            for copy in fills[e + 2]:
                copy.start()

    stores = [pltpu.make_async_copy(out_ref.at[i], r, out_sem.at[i]) for i, r in enumerate(outs)]
    for p in range(4):
        spread = pick_ref[p].astype(F32).T.astype(BF16)
        for n in range(4):
            cut = slice(n * tile, (n + 1) * tile)
            total = dot(spread, back_ref[p, :, cut]).astype(BF16)
            out_ref[2 * p : 2 * p + 2, :, cut] = total.reshape(2, rows, tile)
        stores[2 * p].start()
        stores[2 * p + 1].start()
    for copy in stores:
        copy.wait()


def run_experts(shards, chosen, mine, other, width, capacity):
    local_count, _, hidden = mine[0].shape
    steps = 2 * local_count
    slots = 2 * capacity
    rows, packet = shards[0].shape
    anywhere = pl.BlockSpec(memory_space=pl.ANY)
    return pl.pallas_call(
        functools.partial(expert_kernel, width=width, capacity=capacity, local_count=local_count),
        in_specs=[anywhere] * 8 + [pl.BlockSpec(memory_space=pltpu.VMEM)] + [anywhere] * 6,
        out_specs=[anywhere] * 8,
        out_shape=[jax.ShapeDtypeStruct((rows, width), BF16)] * 8,
        scratch_shapes=[
            pltpu.VMEM((8, rows, packet), BF16),
            pltpu.VMEM((2, width, hidden), BF16),
            pltpu.VMEM((2, width, hidden), BF16),
            pltpu.VMEM((2, hidden, width), BF16),
            pltpu.VMEM((steps, 4 * slots, width), BF16),
            pltpu.VMEM((4, steps * slots, 2 * rows), BF16),
            pltpu.VMEM((steps, 4 * slots, 128), F32),
            pltpu.VMEM((4, steps * slots, width), BF16),
            pltpu.VMEM((8, rows, width), BF16),
            pltpu.SemaphoreType.DMA((8,)),
            pltpu.SemaphoreType.DMA((steps, 3)),
            pltpu.SemaphoreType.DMA((8,)),
        ],
        cost_estimate=pl.CostEstimate(flops=width * hidden, bytes_accessed=rows * width, transcendentals=0),
        compiler_params=pltpu.CompilerParams(vmem_limit_bytes=32 * 2**20),
        name="experts",
    )(*shards, chosen, *mine, *other)


def plus(*parts):
    return sum(p.astype(F32) for p in parts[1:]) + parts[0].astype(F32)


class Links:
    def __init__(self, layout):
        self.layout, self.sent = layout, {}

    def send(self, value, link, turn=1):
        queue = self.sent.setdefault(link, [])
        if len(queue) >= 2:
            value = tie(value, queue[-2])
        queue.append(lax.ppermute(value, AXES, moves(self.layout, **{link: turn})))
        return queue[-1]


def routed_by_gather(layout, place, twin, routed_in, gates, weights, other, capacity):
    rows, width = routed_in.shape
    experts = gates.shape[1]
    local_count = weights[0].shape[0]
    deep = layout[1][2]
    ids = jnp.concatenate([p * local_count + jnp.arange(local_count, dtype=jnp.int32) for p in (place, place ^ twin)])
    ids = jnp.pad(ids, (0, -ids.shape[0] % 8), constant_values=experts)
    chosen = (ids[:, None] == jnp.arange(experts, dtype=jnp.int32)).astype(BF16)
    pad = -(2 * experts) % 128
    chosen = jnp.pad(jnp.concatenate([chosen, chosen], axis=1), ((0, 0), (0, pad)))
    gates_hi, gates_lo = halves(gates)
    packet = jnp.concatenate([routed_in, gates_hi, gates_lo, jnp.zeros((rows, pad), BF16)], axis=1)
    packet = tie(packet, *other)

    links = Links(layout)
    here = {0: packet}
    by_x, by_y, far, sums = {}, {}, {}, {}
    pairs = [(t, t + 1) for t in range(0, deep, 2)]

    def spread(t):
        by_x[t], by_y[t] = links.send(here[t], "x"), links.send(here[t], "y")
        if t + 1 < deep:
            here[t + 1] = links.send(here[t], "z", -1)

    for a, b in pairs:
        if a == 0:
            spread(a)
            spread(b)
        far[a], far[b] = links.send(tie(by_x[a], by_y[b]), "y"), links.send(tie(by_y[b], by_x[b]), "x")
        ahead = [sums[a - 1][0]] if a else []
        if b + 1 < deep:
            spread(b + 1)
            spread(b + 2)
            ahead += [by_x[b + 2], by_y[b + 2]]
        shards = [d[t] for d in (here, by_x, by_y, far) for t in (a, b)]
        done = run_experts([tie(shards[0], *ahead), *shards[1:]], chosen, weights, other, width, capacity)
        sums[a], sums[b] = done[0::2], done[1::2]
    links = Links(layout)

    def own_turn(t, straight, with_far):
        part = plus(sums[t][0], straight, with_far)
        return lax.ppermute(part.astype(BF16), AXES, moves(layout, z=t)) if t else part

    def added(block, back):
        return plus(block, back).astype(BF16)

    back1 = links.send(sums[1][3], "x")
    back0 = links.send(sums[0][3], "y")
    straight1 = links.send(sums[1][1], "x")
    last1 = links.send(added(sums[1][2], back1), "y")
    total = [own_turn(1, straight1, last1)]
    for a, b in pairs[1:]:
        back_b, back_a = links.send(sums[b][3], "x"), links.send(sums[a][3], "y")
        last_a, straight_a = links.send(added(sums[a][1], back_a), "x"), links.send(sums[a][2], "y")
        total.append(own_turn(a, straight_a, last_a))
        straight_b, last_b = links.send(sums[b][1], "x"), links.send(added(sums[b][2], back_b), "y")
        total.append(own_turn(b, straight_b, last_b))
    last0 = links.send(added(tie(sums[0][1], total[0]), back0), "x")
    straight0 = links.send(tie(sums[0][2], total[0]), "y")
    return plus(own_turn(0, straight0, last0), *total)


def routed_by_exchange(routed_in, gates, named, weights, capacity):
    rows, width = routed_in.shape
    expert_gate, expert_up, expert_down = weights
    local_count, experts = expert_gate.shape[0], gates.shape[1]
    count = experts // local_count
    earlier = jnp.dot(jnp.tril(jnp.ones((rows, rows), BF16), -1), named.astype(BF16), preferred_element_type=F32)
    slot = jnp.where(named, earlier.astype(jnp.int32), capacity)
    picks = (slot.T[:, None, :] == jnp.arange(capacity, dtype=jnp.int32)[None, :, None]).reshape(experts * capacity, rows)
    outgoing = jnp.dot(picks.astype(BF16), routed_in, preferred_element_type=F32).astype(BF16)
    received = lax.all_to_all(
        outgoing.reshape(count, local_count, capacity, width), AXES, split_axis=0, concat_axis=0, tiled=True
    )
    received = received.transpose(1, 0, 2, 3).reshape(local_count, count * capacity, width)
    gate_part = jnp.einsum("esd,edf->esf", received, expert_gate, preferred_element_type=F32)
    up_part = jnp.einsum("esd,edf->esf", received, expert_up, preferred_element_type=F32)
    hidden = (jax.nn.silu(gate_part) * up_part).astype(BF16)
    result = jnp.einsum("esf,efd->esd", hidden, expert_down, preferred_element_type=F32).astype(BF16)
    result = result.reshape(local_count, count, capacity, width).transpose(1, 0, 2, 3)
    returned = lax.all_to_all(result, AXES, split_axis=0, concat_axis=0, tiled=True)
    spread = jnp.where(slot[:, :, None] == jnp.arange(capacity, dtype=jnp.int32), gates[:, :, None], 0.0)
    spread_hi, spread_lo = halves(spread.reshape(rows, experts * capacity))
    pulled = jnp.dot(
        jnp.concatenate([spread_hi, spread_lo], axis=0),
        returned.reshape(experts * capacity, width),
        preferred_element_type=F32,
    )
    return pulled[:rows] + pulled[rows:]


def local(
    layout,
    residual,
    mixed_qkv,
    output_gate,
    log_decay,
    write_strength,
    conv_weight,
    norm_gain,
    out_weight,
    post_gain,
    router_weight,
    expert_ids,
    expert_gate,
    expert_up,
    expert_down,
    shared_gate,
    shared_up,
    shared_down,
    shared_switch,
):
    rows, width = residual.shape
    head = norm_gain.shape[0]
    count = lax.axis_size(AXES)
    place = lax.axis_index(AXES)
    before = lax.ppermute(mixed_qkv[rows - 8 :], AXES, [(i, i + 1) for i in range(count - 1)])
    weights = (expert_gate, expert_up, expert_down)
    x, y, z, cores = layout[1]
    twin, facing = flip(layout, core=1), flip(layout, y=1)
    paired = (x, y, cores) == (2, 2, 2) and z % 2 == 0 and twin is not None
    columns = lax.axis_size("exp")
    beside = {i ^ j for i, j in moves_to(layout, lambda c: (c[0], c[1], c[2] ^ 1, c[3]))} if z % 2 == 0 else set()
    near = columns == 4 and None not in (twin, facing) and twin | facing == columns - 1 and len(beside) == 1
    swaps = [lax.ppermute(w, AXES, moves(layout, core=1)) for w in (weights if paired else ())]
    if near:
        swaps.append(lax.ppermute(out_weight, AXES, moves(layout, core=1)))
    block_map, read = delta_terms(mixed_qkv, before, conv_weight, log_decay, write_strength, head)
    half = out_weight.shape[0] // 2
    odd = (place & min(beside)) != 0 if near else None

    some = None
    if near:
        some = jnp.where(odd, out_weight[half:], out_weight[:half])
        some = lax.ppermute(tie(some, before), AXES, moves(layout, y=1))
    state, middle = starting_states(block_map, count, place, some, swaps)
    if near:
        rest = lax.ppermute(tie(some, middle), AXES, moves_to(layout, lambda c: (c[0], c[1], c[2] ^ 1, c[3])))
        out_parts = [[out_weight], [some, rest], swaps[-1:]]
        out_parts.append([lax.ppermute(w, AXES, moves(layout, core=1)) for w in out_parts[1]])
        owners = [(place ^ mask) % columns for mask in (0, facing, twin, facing | twin)]
    normed = emit(read, state, output_gate, norm_gain)
    if near:
        mine = jnp.where(odd, normed[:, half:], normed[:, :half])
        others = jnp.where(odd, normed[:, :half], normed[:, half:])
        products = []
        for part in out_parts:
            by = [normed] if len(part) == 1 else [mine, others]
            products.append(sum(jnp.dot(n, w, preferred_element_type=F32) for n, w in zip(by, part)))
        projected = jnp.concatenate(
            [sum(jnp.where(o == e, p, 0.0) for o, p in zip(owners, products)) for e in range(columns)], axis=1
        )
    else:
        projected = jnp.dot(normed, lax.all_gather(out_weight, "exp", axis=1, tiled=True), preferred_element_type=F32)
    after_mix = (residual.astype(F32) + projected).astype(BF16)
    after_wide = after_mix.astype(F32)
    routed_in = (
        after_wide * lax.rsqrt(jnp.mean(after_wide * after_wide, axis=-1, keepdims=True) + EPS) * post_gain
    ).astype(BF16)

    experts = expert_gate.shape[0] * count
    capacity = rows * expert_ids.shape[1] * 6 // (experts * 5)
    named = jnp.any(expert_ids[:, :, None] == jnp.arange(experts, dtype=jnp.int32), axis=1)
    logits = jnp.dot(routed_in, router_weight, preferred_element_type=F32)
    chosen = jnp.where(named, jnp.exp(jnp.where(named, logits, 0.0)), 0.0)
    gates = chosen / jnp.sum(chosen, axis=1, keepdims=True)
    if paired:
        routed = routed_by_gather(layout, place, twin, routed_in, gates, weights, swaps[:3], capacity)
    else:
        routed = routed_by_exchange(routed_in, gates, named, weights, capacity)
    shared_hidden = (
        jax.nn.silu(jnp.dot(routed_in, shared_gate, preferred_element_type=F32))
        * jnp.dot(routed_in, shared_up, preferred_element_type=F32)
    ).astype(BF16)
    switch = jax.nn.sigmoid(jnp.dot(routed_in, shared_switch, preferred_element_type=F32))
    shared_out = switch[:, None] * jnp.dot(shared_hidden, shared_down, preferred_element_type=F32)
    return (after_wide + routed + shared_out).astype(BF16)


def solution(mesh):
    rows = P(AXES, None)
    return jax.shard_map(
        functools.partial(local, places(mesh)),
        mesh=mesh,
        in_specs=(rows, rows, rows, rows, rows, P(), P(), P(None, "exp"), P(), P(), rows)
        + (P(AXES, None, None),) * 3
        + (P(),) * 4,
        out_specs=rows,
        check_vma=False,
    )
```

```python
import functools

import jax
import jax.numpy as jnp
from jax import lax
from jax.experimental import pallas as pl
from jax.experimental.pallas import tpu as pltpu
from jax.sharding import PartitionSpec as P

AXES = ("ctx", "exp")
EPS = 1e-06
F32, BF16 = jnp.float32, jnp.bfloat16


def dot(a, b, dims=((1,), (0,))):
    return lax.dot_general(a, b, (dims, ((), ())), preferred_element_type=F32)


def halves(x):
    hi = x.astype(BF16)
    return hi, (x - hi.astype(F32)).astype(BF16)


def dot_square(a, b):
    n = b.shape[1]
    ah, al = halves(a)
    bh, bl = halves(b)
    left = jnp.concatenate([ah, al], axis=1)
    right = jnp.concatenate(
        [jnp.concatenate([bh, bl], axis=1), jnp.concatenate([bh, jnp.zeros_like(bl)], axis=1)], axis=0
    )
    both = dot(left, right)
    return both[:, :n] + both[:, n:]


def dot_wide(a, b):
    ah, al = halves(a)
    bh, bl = halves(b)
    return dot(jnp.concatenate([ah, al], axis=1), jnp.concatenate([bh, bh], axis=0)) + dot(ah, bl)


def unit_lower_inverse(lower):
    n = lower[0].shape[0]
    row = lax.broadcasted_iota(jnp.int32, (n, n), 0)
    col = lax.broadcasted_iota(jnp.int32, (n, n), 1)
    eye = jnp.where(row == col, 1.0, 0.0)
    size = 1
    done = None
    while size < n:
        pair = (row // (2 * size) == col // (2 * size)) & (row // size != col // size)
        corner = [jnp.where(pair, m, 0.0) for m in lower]
        if size == 1:
            done = [eye - c for c in corner]
        else:
            half = [dot_square(d, c) for d, c in zip(done, corner)]
            done = [d - dot_square(h, d) for d, h in zip(done, half)]
        size *= 2
    return done


def delta_kernel(q_ref, k_ref, v_ref, qb_ref, kb_ref, vb_ref, qw_ref, kw_ref, vw_ref, cols_ref, rows_ref, map_ref, read_ref, *, head, per):
    rows = q_ref.shape[0]
    groups = q_ref.shape[1] // head

    def conv(x_ref, b_ref, w_ref):
        x = jnp.concatenate([b_ref[...].astype(F32), x_ref[...].astype(F32)], axis=0)
        w = w_ref[...]
        y = w[3:4] * x[8 : 8 + rows]
        for tap in range(3):
            y = y + w[tap : tap + 1] * x[5 + tap : 5 + tap + rows]
        return y / (1.0 + jnp.exp(-y))

    def unit(x):
        return x * lax.rsqrt(jnp.sum(x * x, axis=-1, keepdims=True) + EPS)

    q_all, k_all, v_all = conv(q_ref, qb_ref, qw_ref), conv(k_ref, kb_ref, kw_ref), conv(v_ref, vb_ref, vw_ref)
    row = lax.broadcasted_iota(jnp.int32, (rows, rows), 0)
    col = lax.broadcasted_iota(jnp.int32, (rows, rows), 1)
    lower, info = [], []
    for g in range(groups):
        q = unit(q_all[:, g * head : (g + 1) * head]) * head**-0.5
        k = unit(k_all[:, g * head : (g + 1) * head])
        kh, kl = halves(k)
        qh, ql = halves(q)
        top = jnp.concatenate([jnp.concatenate([kh, kl], axis=1), jnp.concatenate([qh, ql], axis=1)], axis=0)
        inner = dot(top, jnp.concatenate([kh, kh], axis=1), ((1,), (1,)))
        inner = inner + dot(jnp.concatenate([kh, qh], axis=0), kl, ((1,), (1,)))
        kk, qk = inner[:rows], inner[rows:]
        for i in range(per):
            j = g * per + i
            cum_col = cols_ref[j, :, 0:1]
            strength = cols_ref[j, :, 1:2]
            cum_row = rows_ref[j, 0:1, :]
            gap = cum_col - cum_row
            ratios = jnp.where(row >= col, jnp.exp(jnp.where(row >= col, gap, 0.0)), 0.0)
            lower.append(jnp.where(row > col, ratios * kk, 0.0) * strength)
            info.append((q, k, v_all[:, j * head : (j + 1) * head], cum_col, strength, qk * ratios))
    inverse = unit_lower_inverse(lower)
    for j, (q, k, v, cum, strength, scores) in enumerate(info):
        decay = jnp.exp(cum)
        right = jnp.concatenate([strength * decay * k, strength * v], axis=1)
        solved = dot_wide(inverse[j], right)
        last = cum[rows - 1 : rows]
        to_end = k * jnp.exp(last - cum)
        update = dot_wide(to_end.T, solved)
        end = jnp.exp(last)
        diag = lax.broadcasted_iota(jnp.int32, (head, head), 0) == lax.broadcasted_iota(jnp.int32, (head, head), 1)
        map_ref[j, :, :head] = jnp.where(diag, end, 0.0) - update[:, :head]
        map_ref[j, :, head:] = update[:, head:]
        read = dot_wide(scores, solved)
        read_ref[j, :, :head] = q * decay - read[:, :head]
        read_ref[j, :, head:] = read[:, head:]


def delta_terms(mixed, before, conv_weight, log_decay, write_strength, head):
    rows, vheads = log_decay.shape
    kheads = (mixed.shape[1] // head - vheads) // 2
    per = vheads // kheads
    together = 2 if kheads % 2 == 0 else 1
    steps = kheads // together
    causal = jnp.tril(jnp.ones((rows, rows), F32))
    cumul = jnp.dot(causal, log_decay, precision=lax.Precision.HIGHEST)
    cols = jnp.stack([cumul.T, write_strength.T], axis=2)
    lines = cumul.T[:, None, :]
    qw, vw = together * head, together * per * head
    k_at, v_at = kheads * head // qw, 2 * kheads * head // vw

    def spec(height, width, at):
        return pl.BlockSpec((height, width), lambda s: (0, s + at))

    n = together * per
    return pl.pallas_call(
        functools.partial(delta_kernel, head=head, per=per),
        grid=(steps,),
        in_specs=[spec(h, w, a) for h in (rows, 8, 4) for w, a in ((qw, 0), (qw, k_at), (vw, v_at))]
        + [
            pl.BlockSpec((n, rows, 2), lambda s: (s, 0, 0)),
            pl.BlockSpec((n, 1, rows), lambda s: (s, 0, 0)),
        ],
        out_specs=[pl.BlockSpec((n, head, 2 * head), lambda s: (s, 0, 0)), pl.BlockSpec((n, rows, 2 * head), lambda s: (s, 0, 0))],
        out_shape=[jax.ShapeDtypeStruct((vheads, head, 2 * head), F32), jax.ShapeDtypeStruct((vheads, rows, 2 * head), F32)],
        cost_estimate=pl.CostEstimate(flops=rows * head * head * vheads, bytes_accessed=rows * head * vheads, transcendentals=0),
        compiler_params=pltpu.CompilerParams(vmem_limit_bytes=40 * 2**20),
        name="delta_terms",
    )(mixed, mixed, mixed, before, before, before, conv_weight, conv_weight, conv_weight, cols, lines)


def emit_kernel(read_ref, state_ref, gate_ref, gain_ref, out_ref):
    n, rows, head2 = read_ref.shape
    head = head2 // 2
    for j in range(n):
        out = dot_square(read_ref[j, :, :head], state_ref[j]) + read_ref[j, :, head:]
        normed = out * lax.rsqrt(jnp.mean(out * out, axis=-1, keepdims=True) + EPS)
        gate = gate_ref[:, j * head : (j + 1) * head].astype(F32)
        out_ref[:, j * head : (j + 1) * head] = (normed * gain_ref[...] * (gate / (1.0 + jnp.exp(-gate)))).astype(BF16)


def emit(read, state, output_gate, gain):
    vheads, rows, head2 = read.shape
    head = head2 // 2
    n = 4 if vheads % 4 == 0 else 1
    return pl.pallas_call(
        emit_kernel,
        grid=(vheads // n,),
        in_specs=[
            pl.BlockSpec((n, rows, head2), lambda s: (s, 0, 0)),
            pl.BlockSpec((n, head, head), lambda s: (s, 0, 0)),
            pl.BlockSpec((rows, n * head), lambda s: (0, s)),
            pl.BlockSpec((1, head), lambda s: (0, 0)),
        ],
        out_specs=pl.BlockSpec((rows, n * head), lambda s: (0, s)),
        out_shape=jax.ShapeDtypeStruct((rows, vheads * head), BF16),
        name="emit",
    )(read, state, output_gate, gain[None])


def tie(value, *after):
    return lax.optimization_barrier((value, *after))[0]


def apply(transform, right):
    return jnp.einsum("hij,hjk->hik", transform, right, precision=lax.Precision.HIGHEST)


def starting_states(block_map, count, place, ready, swaps):
    head = block_map.shape[1]
    levels, step = [], 1
    held = block_map
    while count % (2 * step) == 0 and 4 * step < count and held.shape[0] % 2 == 0:
        share = held.shape[0] // 2
        upper = (place // step) % 2 == 1
        keep = jnp.where(upper, held[share:], held[:share])
        give = jnp.where(upper, held[:share], held[share:])
        kind = F32 if step == 1 else BF16
        if step == 1 and ready is not None:
            give = tie(give, *ready)
        got = lax.ppermute(give.astype(kind), AXES, [(i, i ^ step) for i in range(count)]).astype(F32)
        early, late = jnp.where(upper, got, keep), jnp.where(upper, keep, got)
        merged = apply(late[:, :, :head], early)
        held = jnp.concatenate([merged[:, :, :head], merged[:, :, head:] + late[:, :, head:]], axis=2)
        levels.append((step, upper, early))
        step *= 2
    state = jnp.zeros_like(held[:, :, head:])
    for turn in range(count // step - 1):
        ahead = held[:, :, head:]
        if turn:
            ahead = ahead + apply(held[:, :, :head], state)
        state = lax.ppermute(ahead.astype(BF16), AXES, [(i, i + step) for i in range(count - step)]).astype(F32)
    middle = state
    state = tie(state, *swaps)
    for step, upper, early in reversed(levels):
        second = apply(early[:, :, :head], state) + early[:, :, head:]
        mine, other = jnp.where(upper, second, state), jnp.where(upper, state, second)
        got = lax.ppermute(other.astype(BF16), AXES, [(i, i ^ step) for i in range(count)]).astype(F32)
        state = jnp.where(upper, jnp.concatenate([got, mine], axis=0), jnp.concatenate([mine, got], axis=0))
    return state, middle


def places(mesh):
    at = {(*d.coords, d.core_on_chip): i for i, d in enumerate(mesh.devices.flat)}
    return at, tuple(max(c[k] for c in at) + 1 for k in range(4))


def moves_to(layout, target):
    at, _ = layout
    return [(i, at[target(spot)]) for spot, i in at.items()]


def moves(layout, x=0, y=0, z=0, core=0):
    at, size = layout
    shift = (x, y, z, core)
    return [(i, at[tuple((c + s) % n for c, s, n in zip(spot, shift, size))]) for spot, i in at.items()]


def flip(layout, **by):
    masks = {i ^ j for i, j in moves(layout, **by)}
    return masks.pop() if len(masks) == 1 else None


def expert_kernel(*refs, width, capacity, local_count):
    shards, (chosen_ref, *weights), outs = refs[:8], refs[8:15], refs[15:23]
    block_ref, gate_w, up_w, down_w, sel_ref, pick_ref, gate_ref, back_ref, out_ref, in_sem, w_sem, out_sem = refs[23:]
    steps = 2 * local_count
    rows = shards[0].shape[0]
    pair_rows, slots = 2 * rows, 2 * capacity
    tile = width // 4
    packet = shards[0].shape[1]

    loads = [pltpu.make_async_copy(r, block_ref.at[i], in_sem.at[i]) for i, r in enumerate(shards)]
    fills = []
    for e in range(steps):
        part = weights[:3] if e < local_count else weights[3:]
        fills.append(
            [
                pltpu.make_async_copy(r.at[e % local_count], w.at[e % 2], w_sem.at[e, k])
                for k, (r, w) in enumerate(zip(part, (gate_w, up_w, down_w)))
            ]
        )
    for copy in loads + fills[0] + fills[1]:
        copy.start()

    before = lax.broadcasted_iota(jnp.int32, (pair_rows, pair_rows), 0)
    after = lax.broadcasted_iota(jnp.int32, (pair_rows, pair_rows), 1)
    earlier = jnp.where((before < after) & (before // rows == after // rows), 1.0, 0.0).astype(BF16)
    second = lax.broadcasted_iota(jnp.int32, (1, pair_rows), 1) // rows
    slot = lax.broadcasted_iota(jnp.int32, (slots, pair_rows), 0)
    for p in range(4):
        loads[2 * p].wait()
        loads[2 * p + 1].wait()
        marks = block_ref[2 * p : 2 * p + 2, :, width:].reshape(pair_rows, packet - width)
        gates = dot(chosen_ref[...], marks, ((1,), (1,)))
        named = jnp.where(gates != 0.0, 1.0, 0.0)
        rank = dot(named.astype(BF16), earlier).astype(jnp.int32)
        spot = jnp.where(gates != 0.0, rank + second * capacity, -1)
        for e in range(steps):
            hit = slot == spot[e : e + 1]
            pick_ref[p, e * slots : (e + 1) * slots, :] = jnp.where(hit, 1.0, 0.0).astype(BF16)
            gate = jnp.sum(jnp.where(hit, gates[e : e + 1], 0.0), axis=1, keepdims=True)
            gate_ref[e, p * slots : (p + 1) * slots, :] = jnp.broadcast_to(gate, (slots, 128))
        for n in range(4):
            cut = slice(n * tile, (n + 1) * tile)
            taken = dot(pick_ref[p], block_ref[2 * p : 2 * p + 2, :, cut].reshape(pair_rows, tile)).astype(BF16)
            for e in range(steps):
                sel_ref[e, p * slots : (p + 1) * slots, cut] = taken[e * slots : (e + 1) * slots]

    for e in range(steps):
        for copy in fills[e]:
            copy.wait()
        rows_in = sel_ref[e]
        gate, up = dot(rows_in, gate_w[e % 2]), dot(rows_in, up_w[e % 2])
        hidden = (gate / (1.0 + jnp.exp(-gate)) * up).astype(BF16)
        weight = gate_ref[e][:, 0:1]
        for n in range(4):
            cut = slice(n * tile, (n + 1) * tile)
            result = (dot(hidden, down_w[e % 2, :, cut]) * weight).astype(BF16)
            for p in range(4):
                back_ref[p, e * slots : (e + 1) * slots, cut] = result[p * slots : (p + 1) * slots]
        if e + 2 < steps:
            for copy in fills[e + 2]:
                copy.start()

    stores = [pltpu.make_async_copy(out_ref.at[i], r, out_sem.at[i]) for i, r in enumerate(outs)]
    for p in range(4):
        spread = pick_ref[p].astype(F32).T.astype(BF16)
        for n in range(4):
            cut = slice(n * tile, (n + 1) * tile)
            total = dot(spread, back_ref[p, :, cut]).astype(BF16)
            out_ref[2 * p : 2 * p + 2, :, cut] = total.reshape(2, rows, tile)
        stores[2 * p].start()
        stores[2 * p + 1].start()
    for copy in stores:
        copy.wait()


def run_experts(shards, chosen, mine, other, width, capacity):
    local_count, _, hidden = mine[0].shape
    steps = 2 * local_count
    slots = 2 * capacity
    rows, packet = shards[0].shape
    anywhere = pl.BlockSpec(memory_space=pl.ANY)
    return pl.pallas_call(
        functools.partial(expert_kernel, width=width, capacity=capacity, local_count=local_count),
        in_specs=[anywhere] * 8 + [pl.BlockSpec(memory_space=pltpu.VMEM)] + [anywhere] * 6,
        out_specs=[anywhere] * 8,
        out_shape=[jax.ShapeDtypeStruct((rows, width), BF16)] * 8,
        scratch_shapes=[
            pltpu.VMEM((8, rows, packet), BF16),
            pltpu.VMEM((2, width, hidden), BF16),
            pltpu.VMEM((2, width, hidden), BF16),
            pltpu.VMEM((2, hidden, width), BF16),
            pltpu.VMEM((steps, 4 * slots, width), BF16),
            pltpu.VMEM((4, steps * slots, 2 * rows), BF16),
            pltpu.VMEM((steps, 4 * slots, 128), F32),
            pltpu.VMEM((4, steps * slots, width), BF16),
            pltpu.VMEM((8, rows, width), BF16),
            pltpu.SemaphoreType.DMA((8,)),
            pltpu.SemaphoreType.DMA((steps, 3)),
            pltpu.SemaphoreType.DMA((8,)),
        ],
        cost_estimate=pl.CostEstimate(flops=width * hidden, bytes_accessed=rows * width, transcendentals=0),
        compiler_params=pltpu.CompilerParams(vmem_limit_bytes=32 * 2**20),
        name="experts",
    )(*shards, chosen, *mine, *other)


def plus(*parts):
    return sum(p.astype(F32) for p in parts[1:]) + parts[0].astype(F32)


def project_kernel(spots_ref, normed_ref, residual_ref, gain_ref, *refs, counts):
    parts, (mix_ref, routed_ref, sum_ref) = refs[:-3], refs[-3:]
    depth = normed_ref.shape[1]
    half = depth // 2
    low, high = normed_ref[:, :half], normed_ref[:, half:]
    odd = spots_ref[len(counts)] == 1
    mine, others = jnp.where(odd, high, low), jnp.where(odd, low, high)
    ordered = jnp.concatenate([mine, others], axis=1)
    first = 0
    for k, n in enumerate(counts):
        left = normed_ref[...] if n == 1 else ordered
        total, at = None, 0
        for w_ref in parts[first : first + n]:
            rows = w_ref.shape[0]
            product = dot(left[:, at : at + rows], w_ref[...])
            total = product if total is None else total + product
            at += rows
        first += n
        width = total.shape[1]
        sum_ref[:, pl.ds(pl.multiple_of(spots_ref[k] * width, width), width)] = total
    mix = (residual_ref[...].astype(F32) + sum_ref[...]).astype(BF16)
    mix_ref[...] = mix
    wide = mix.astype(F32)
    scale = lax.rsqrt(jnp.mean(wide * wide, axis=-1, keepdims=True) + EPS)
    routed_ref[...] = (wide * scale * gain_ref[...]).astype(BF16)


def project(spots, normed, residual, gain, parts):
    vmem = pl.BlockSpec(memory_space=pltpu.VMEM)
    flat = sum(parts, [])
    return pl.pallas_call(
        functools.partial(project_kernel, counts=[len(p) for p in parts]),
        in_specs=[pl.BlockSpec(memory_space=pltpu.SMEM)] + [vmem] * (3 + len(flat)),
        out_specs=[vmem] * 2,
        out_shape=[jax.ShapeDtypeStruct(residual.shape, BF16)] * 2,
        scratch_shapes=[pltpu.VMEM(residual.shape, F32)],
        cost_estimate=pl.CostEstimate(flops=1, bytes_accessed=residual.size, transcendentals=0),
        compiler_params=pltpu.CompilerParams(vmem_limit_bytes=24 * 2**20),
        name="project",
    )(spots, normed, residual, gain[None], *flat)


class Links:
    def __init__(self, layout):
        self.layout, self.sent = layout, {}

    def send(self, value, link, turn=1):
        queue = self.sent.setdefault(link, [])
        if len(queue) >= 2:
            value = tie(value, queue[-2])
        queue.append(lax.ppermute(value, AXES, moves(self.layout, **{link: turn})))
        return queue[-1]


def routed_by_gather(layout, place, twin, routed_in, gates, weights, other, capacity):
    rows, width = routed_in.shape
    experts = gates.shape[1]
    local_count = weights[0].shape[0]
    deep = layout[1][2]
    ids = jnp.concatenate([p * local_count + jnp.arange(local_count, dtype=jnp.int32) for p in (place, place ^ twin)])
    ids = jnp.pad(ids, (0, -ids.shape[0] % 8), constant_values=experts)
    chosen = (ids[:, None] == jnp.arange(experts, dtype=jnp.int32)).astype(BF16)
    pad = -(2 * experts) % 128
    chosen = jnp.pad(jnp.concatenate([chosen, chosen], axis=1), ((0, 0), (0, pad)))
    gates_hi, gates_lo = halves(gates)
    packet = jnp.concatenate([routed_in, gates_hi, gates_lo, jnp.zeros((rows, pad), BF16)], axis=1)
    packet = tie(packet, *other)

    links = Links(layout)
    here = {0: packet}
    by_x, by_y, far, sums = {}, {}, {}, {}
    pairs = [(t, t + 1) for t in range(0, deep, 2)]

    def spread(t):
        by_x[t], by_y[t] = links.send(here[t], "x"), links.send(here[t], "y")
        if t + 1 < deep:
            here[t + 1] = links.send(here[t], "z", -1)

    for a, b in pairs:
        if a == 0:
            spread(a)
            spread(b)
        far[a], far[b] = links.send(tie(by_x[a], by_y[b]), "y"), links.send(tie(by_y[b], by_x[b]), "x")
        ahead = [sums[a - 1][0]] if a else []
        if b + 1 < deep:
            spread(b + 1)
            spread(b + 2)
            ahead += [by_x[b + 2], by_y[b + 2]]
        shards = [d[t] for d in (here, by_x, by_y, far) for t in (a, b)]
        done = run_experts([tie(shards[0], *ahead), *shards[1:]], chosen, weights, other, width, capacity)
        sums[a], sums[b] = done[0::2], done[1::2]
    links = Links(layout)

    def own_turn(t, straight, with_far):
        part = plus(sums[t][0], straight, with_far)
        return lax.ppermute(part.astype(BF16), AXES, moves(layout, z=t)) if t else part

    def added(block, back):
        return plus(block, back).astype(BF16)

    back1 = links.send(sums[1][3], "x")
    back0 = links.send(tie(sums[0][3], back1), "y")
    straight1 = links.send(tie(sums[1][1], back1), "x")
    last1 = links.send(added(sums[1][2], back1), "y")
    total = [own_turn(1, straight1, last1)]
    for a, b in pairs[1:]:
        back_b, back_a = links.send(sums[b][3], "x"), links.send(sums[a][3], "y")
        last_a, straight_a = links.send(added(sums[a][1], back_a), "x"), links.send(sums[a][2], "y")
        total.append(own_turn(a, straight_a, last_a))
        straight_b, last_b = links.send(sums[b][1], "x"), links.send(added(sums[b][2], back_b), "y")
        total.append(own_turn(b, straight_b, last_b))
    last0 = links.send(added(tie(sums[0][1], total[0]), back0), "x")
    straight0 = links.send(tie(sums[0][2], total[0]), "y")
    return plus(own_turn(0, straight0, last0), *total)


def routed_by_exchange(routed_in, gates, named, weights, capacity):
    rows, width = routed_in.shape
    expert_gate, expert_up, expert_down = weights
    local_count, experts = expert_gate.shape[0], gates.shape[1]
    count = experts // local_count
    earlier = jnp.dot(jnp.tril(jnp.ones((rows, rows), BF16), -1), named.astype(BF16), preferred_element_type=F32)
    slot = jnp.where(named, earlier.astype(jnp.int32), capacity)
    picks = (slot.T[:, None, :] == jnp.arange(capacity, dtype=jnp.int32)[None, :, None]).reshape(experts * capacity, rows)
    outgoing = jnp.dot(picks.astype(BF16), routed_in, preferred_element_type=F32).astype(BF16)
    received = lax.all_to_all(
        outgoing.reshape(count, local_count, capacity, width), AXES, split_axis=0, concat_axis=0, tiled=True
    )
    received = received.transpose(1, 0, 2, 3).reshape(local_count, count * capacity, width)
    gate_part = jnp.einsum("esd,edf->esf", received, expert_gate, preferred_element_type=F32)
    up_part = jnp.einsum("esd,edf->esf", received, expert_up, preferred_element_type=F32)
    hidden = (jax.nn.silu(gate_part) * up_part).astype(BF16)
    result = jnp.einsum("esf,efd->esd", hidden, expert_down, preferred_element_type=F32).astype(BF16)
    result = result.reshape(local_count, count, capacity, width).transpose(1, 0, 2, 3)
    returned = lax.all_to_all(result, AXES, split_axis=0, concat_axis=0, tiled=True)
    spread = jnp.where(slot[:, :, None] == jnp.arange(capacity, dtype=jnp.int32), gates[:, :, None], 0.0)
    spread_hi, spread_lo = halves(spread.reshape(rows, experts * capacity))
    pulled = jnp.dot(
        jnp.concatenate([spread_hi, spread_lo], axis=0),
        returned.reshape(experts * capacity, width),
        preferred_element_type=F32,
    )
    return pulled[:rows] + pulled[rows:]


def local(
    layout,
    residual,
    mixed_qkv,
    output_gate,
    log_decay,
    write_strength,
    conv_weight,
    norm_gain,
    out_weight,
    post_gain,
    router_weight,
    expert_ids,
    expert_gate,
    expert_up,
    expert_down,
    shared_gate,
    shared_up,
    shared_down,
    shared_switch,
):
    rows, width = residual.shape
    head = norm_gain.shape[0]
    count = lax.axis_size(AXES)
    place = lax.axis_index(AXES)
    before = lax.ppermute(mixed_qkv[rows - 8 :], AXES, [(i, i + 1) for i in range(count - 1)])
    weights = (expert_gate, expert_up, expert_down)
    x, y, z, cores = layout[1]
    twin, facing = flip(layout, core=1), flip(layout, y=1)
    paired = (x, y, cores) == (2, 2, 2) and z % 2 == 0 and twin is not None
    columns = lax.axis_size("exp")
    beside = {i ^ j for i, j in moves_to(layout, lambda c: (c[0], c[1], c[2] ^ 1, c[3]))} if z % 2 == 0 else set()
    along = flip(layout, x=1)
    near = columns == 4 and None not in (twin, facing, along) and twin | facing == columns - 1 and len(beside) == 1
    swaps = [lax.ppermute(w, AXES, moves(layout, core=1)) for w in (weights if paired else ())]
    if near:
        swaps.append(lax.ppermute(out_weight, AXES, moves(layout, core=1)))
    block_map, read = delta_terms(mixed_qkv, before, conv_weight, log_decay, write_strength, head)
    half = out_weight.shape[0] // 2
    quarter = half // 2
    odd = ((place & min(beside)) != 0) ^ ((place & along) != 0) if near else None

    some = None
    if near:
        some = jnp.where(odd, out_weight[half:], out_weight[:half])
        some = [
            lax.ppermute(w, AXES, moves(layout, y=1))
            for w in lax.optimization_barrier((some[:quarter], some[quarter:], before))[:2]
        ]
    state, middle = starting_states(block_map, count, place, some, swaps)
    if near:
        pieces = tie(some[0], middle), tie(some[1], middle)
        rest = [
            lax.ppermute(pieces[0], AXES, moves(layout, x=1)),
            lax.ppermute(pieces[1], AXES, moves_to(layout, lambda c: (c[0], c[1], c[2] ^ 1, c[3]))),
        ]
        out_parts = [[out_weight], [*some, *rest], swaps[-1:]]
        out_parts.append([lax.ppermute(w, AXES, moves(layout, core=1)) for w in out_parts[1]])
        owners = [(place ^ mask) % columns for mask in (0, facing, twin, facing | twin)]
    normed = emit(read, state, output_gate, norm_gain)
    if near:
        spots = jnp.stack([jnp.int32(o) for o in owners] + [odd.astype(jnp.int32)])
        after_mix, routed_in = project(spots, normed, residual, post_gain, out_parts)
    else:
        projected = jnp.dot(normed, lax.all_gather(out_weight, "exp", axis=1, tiled=True), preferred_element_type=F32)
        after_mix = (residual.astype(F32) + projected).astype(BF16)
        after_wide = after_mix.astype(F32)
        scale = lax.rsqrt(jnp.mean(after_wide * after_wide, axis=-1, keepdims=True) + EPS)
        routed_in = (after_wide * scale * post_gain).astype(BF16)
    after_wide = after_mix.astype(F32)

    experts = expert_gate.shape[0] * count
    capacity = rows * expert_ids.shape[1] * 6 // (experts * 5)
    named = jnp.any(expert_ids[:, :, None] == jnp.arange(experts, dtype=jnp.int32), axis=1)
    logits = jnp.dot(routed_in, router_weight, preferred_element_type=F32)
    chosen = jnp.where(named, jnp.exp(jnp.where(named, logits, 0.0)), 0.0)
    gates = chosen / jnp.sum(chosen, axis=1, keepdims=True)
    if paired:
        routed = routed_by_gather(layout, place, twin, routed_in, gates, weights, swaps[:3], capacity)
    else:
        routed = routed_by_exchange(routed_in, gates, named, weights, capacity)
    shared_hidden = (
        jax.nn.silu(jnp.dot(routed_in, shared_gate, preferred_element_type=F32))
        * jnp.dot(routed_in, shared_up, preferred_element_type=F32)
    ).astype(BF16)
    switch = jax.nn.sigmoid(jnp.dot(routed_in, shared_switch, preferred_element_type=F32))
    shared_out = switch[:, None] * jnp.dot(shared_hidden, shared_down, preferred_element_type=F32)
    return (after_wide + routed + shared_out).astype(BF16)


def solution(mesh):
    rows = P(AXES, None)
    return jax.shard_map(
        functools.partial(local, places(mesh)),
        mesh=mesh,
        in_specs=(rows, rows, rows, rows, rows, P(), P(), P(None, "exp"), P(), P(), rows)
        + (P(AXES, None, None),) * 3
        + (P(),) * 4,
        out_specs=rows,
        check_vma=False,
    )
```

```python
import functools

import jax
import jax.numpy as jnp
from jax import lax
from jax.experimental import pallas as pl
from jax.experimental.pallas import tpu as pltpu
from jax.sharding import PartitionSpec as P

AXES = ("ctx", "exp")
EPS = 1e-06
F32, BF16 = jnp.float32, jnp.bfloat16


def dot(a, b, dims=((1,), (0,))):
    return lax.dot_general(a, b, (dims, ((), ())), preferred_element_type=F32)


def halves(x):
    hi = x.astype(BF16)
    return hi, (x - hi.astype(F32)).astype(BF16)


def dot_square(a, b):
    n = b.shape[1]
    ah, al = halves(a)
    bh, bl = halves(b)
    left = jnp.concatenate([ah, al], axis=1)
    right = jnp.concatenate(
        [jnp.concatenate([bh, bl], axis=1), jnp.concatenate([bh, jnp.zeros_like(bl)], axis=1)], axis=0
    )
    both = dot(left, right)
    return both[:, :n] + both[:, n:]


def dot_wide(a, b):
    ah, al = halves(a)
    bh, bl = halves(b)
    return dot(jnp.concatenate([ah, al], axis=1), jnp.concatenate([bh, bh], axis=0)) + dot(ah, bl)


def unit_lower_inverse(lower):
    n = lower[0].shape[0]
    row = lax.broadcasted_iota(jnp.int32, (n, n), 0)
    col = lax.broadcasted_iota(jnp.int32, (n, n), 1)
    eye = jnp.where(row == col, 1.0, 0.0)
    size = 1
    done = None
    while size < n:
        pair = (row // (2 * size) == col // (2 * size)) & (row // size != col // size)
        corner = [jnp.where(pair, m, 0.0) for m in lower]
        if size == 1:
            done = [eye - c for c in corner]
        else:
            half = [dot_square(d, c) for d, c in zip(done, corner)]
            done = [d - dot_square(h, d) for d, h in zip(done, half)]
        size *= 2
    return done


def delta_kernel(q_ref, k_ref, v_ref, qb_ref, kb_ref, vb_ref, qw_ref, kw_ref, vw_ref, cols_ref, rows_ref, map_ref, read_ref, *, head, per):
    rows = q_ref.shape[0]
    groups = q_ref.shape[1] // head

    def conv(x_ref, b_ref, w_ref):
        x = jnp.concatenate([b_ref[...].astype(F32), x_ref[...].astype(F32)], axis=0)
        w = w_ref[...]
        y = w[3:4] * x[8 : 8 + rows]
        for tap in range(3):
            y = y + w[tap : tap + 1] * x[5 + tap : 5 + tap + rows]
        return y / (1.0 + jnp.exp(-y))

    def unit(x):
        return x * lax.rsqrt(jnp.sum(x * x, axis=-1, keepdims=True) + EPS)

    q_all, k_all, v_all = conv(q_ref, qb_ref, qw_ref), conv(k_ref, kb_ref, kw_ref), conv(v_ref, vb_ref, vw_ref)
    row = lax.broadcasted_iota(jnp.int32, (rows, rows), 0)
    col = lax.broadcasted_iota(jnp.int32, (rows, rows), 1)
    lower, info = [], []
    for g in range(groups):
        q = unit(q_all[:, g * head : (g + 1) * head]) * head**-0.5
        k = unit(k_all[:, g * head : (g + 1) * head])
        kh, kl = halves(k)
        qh, ql = halves(q)
        top = jnp.concatenate([jnp.concatenate([kh, kl], axis=1), jnp.concatenate([qh, ql], axis=1)], axis=0)
        inner = dot(top, jnp.concatenate([kh, kh], axis=1), ((1,), (1,)))
        inner = inner + dot(jnp.concatenate([kh, qh], axis=0), kl, ((1,), (1,)))
        kk, qk = inner[:rows], inner[rows:]
        for i in range(per):
            j = g * per + i
            cum_col = cols_ref[j, :, 0:1]
            strength = cols_ref[j, :, 1:2]
            cum_row = rows_ref[j, 0:1, :]
            gap = cum_col - cum_row
            ratios = jnp.where(row >= col, jnp.exp(jnp.where(row >= col, gap, 0.0)), 0.0)
            lower.append(jnp.where(row > col, ratios * kk, 0.0) * strength)
            info.append((q, k, v_all[:, j * head : (j + 1) * head], cum_col, strength, qk * ratios))
    inverse = unit_lower_inverse(lower)
    for j, (q, k, v, cum, strength, scores) in enumerate(info):
        decay = jnp.exp(cum)
        right = jnp.concatenate([strength * decay * k, strength * v], axis=1)
        solved = dot_wide(inverse[j], right)
        last = cum[rows - 1 : rows]
        to_end = k * jnp.exp(last - cum)
        update = dot_wide(to_end.T, solved)
        end = jnp.exp(last)
        diag = lax.broadcasted_iota(jnp.int32, (head, head), 0) == lax.broadcasted_iota(jnp.int32, (head, head), 1)
        map_ref[j, :, :head] = jnp.where(diag, end, 0.0) - update[:, :head]
        map_ref[j, :, head:] = update[:, head:]
        read = dot_wide(scores, solved)
        read_ref[j, :, :head] = q * decay - read[:, :head]
        read_ref[j, :, head:] = read[:, head:]


def delta_terms(mixed, before, conv_weight, log_decay, write_strength, head):
    rows, vheads = log_decay.shape
    kheads = (mixed.shape[1] // head - vheads) // 2
    per = vheads // kheads
    together = 2 if kheads % 2 == 0 else 1
    steps = kheads // together
    causal = jnp.tril(jnp.ones((rows, rows), F32))
    cumul = jnp.dot(causal, log_decay, precision=lax.Precision.HIGHEST)
    cols = jnp.stack([cumul.T, write_strength.T], axis=2)
    lines = cumul.T[:, None, :]
    qw, vw = together * head, together * per * head
    k_at, v_at = kheads * head // qw, 2 * kheads * head // vw

    def spec(height, width, at):
        return pl.BlockSpec((height, width), lambda s: (0, s + at))

    n = together * per
    return pl.pallas_call(
        functools.partial(delta_kernel, head=head, per=per),
        grid=(steps,),
        in_specs=[spec(h, w, a) for h in (rows, 8, 4) for w, a in ((qw, 0), (qw, k_at), (vw, v_at))]
        + [
            pl.BlockSpec((n, rows, 2), lambda s: (s, 0, 0)),
            pl.BlockSpec((n, 1, rows), lambda s: (s, 0, 0)),
        ],
        out_specs=[pl.BlockSpec((n, head, 2 * head), lambda s: (s, 0, 0)), pl.BlockSpec((n, rows, 2 * head), lambda s: (s, 0, 0))],
        out_shape=[jax.ShapeDtypeStruct((vheads, head, 2 * head), F32), jax.ShapeDtypeStruct((vheads, rows, 2 * head), F32)],
        cost_estimate=pl.CostEstimate(flops=rows * head * head * vheads, bytes_accessed=rows * head * vheads, transcendentals=0),
        compiler_params=pltpu.CompilerParams(vmem_limit_bytes=40 * 2**20),
        name="delta_terms",
    )(mixed, mixed, mixed, before, before, before, conv_weight, conv_weight, conv_weight, cols, lines)


def emit_kernel(read_ref, state_ref, gate_ref, gain_ref, out_ref):
    n, rows, head2 = read_ref.shape
    head = head2 // 2
    for j in range(n):
        out = dot_square(read_ref[j, :, :head], state_ref[j]) + read_ref[j, :, head:]
        normed = out * lax.rsqrt(jnp.mean(out * out, axis=-1, keepdims=True) + EPS)
        gate = gate_ref[:, j * head : (j + 1) * head].astype(F32)
        out_ref[:, j * head : (j + 1) * head] = (normed * gain_ref[...] * (gate / (1.0 + jnp.exp(-gate)))).astype(BF16)


def emit(read, state, output_gate, gain):
    vheads, rows, head2 = read.shape
    head = head2 // 2
    n = 8 if vheads % 8 == 0 else 1
    return pl.pallas_call(
        emit_kernel,
        grid=(vheads // n,),
        in_specs=[
            pl.BlockSpec((n, rows, head2), lambda s: (s, 0, 0)),
            pl.BlockSpec((n, head, head), lambda s: (s, 0, 0)),
            pl.BlockSpec((rows, n * head), lambda s: (0, s)),
            pl.BlockSpec((1, head), lambda s: (0, 0)),
        ],
        out_specs=pl.BlockSpec((rows, n * head), lambda s: (0, s)),
        out_shape=jax.ShapeDtypeStruct((rows, vheads * head), BF16),
        name="emit",
    )(read, state, output_gate, gain[None])


def tie(value, *after):
    return lax.optimization_barrier((value, *after))[0]


def apply(transform, right):
    return jnp.einsum("hij,hjk->hik", transform, right, precision=lax.Precision.HIGHEST)


def starting_states(block_map, count, place, ready, swaps):
    head = block_map.shape[1]
    levels, step = [], 1
    held = block_map
    while count % (2 * step) == 0 and 4 * step < count and held.shape[0] % 2 == 0:
        share = held.shape[0] // 2
        upper = (place // step) % 2 == 1
        keep = jnp.where(upper, held[share:], held[:share])
        give = jnp.where(upper, held[:share], held[share:])
        kind = F32 if step == 1 else BF16
        if step == 1 and ready is not None:
            give = tie(give, *ready)
        got = lax.ppermute(give.astype(kind), AXES, [(i, i ^ step) for i in range(count)]).astype(F32)
        early, late = jnp.where(upper, got, keep), jnp.where(upper, keep, got)
        merged = apply(late[:, :, :head], early)
        held = jnp.concatenate([merged[:, :, :head], merged[:, :, head:] + late[:, :, head:]], axis=2)
        levels.append((step, upper, early))
        step *= 2
    state = jnp.zeros_like(held[:, :, head:])
    for turn in range(count // step - 1):
        ahead = held[:, :, head:]
        if turn:
            ahead = ahead + apply(held[:, :, :head], state)
        state = lax.ppermute(ahead.astype(BF16), AXES, [(i, i + step) for i in range(count - step)]).astype(F32)
    middle = state
    state = tie(state, *swaps)
    for step, upper, early in reversed(levels):
        second = apply(early[:, :, :head], state) + early[:, :, head:]
        mine, other = jnp.where(upper, second, state), jnp.where(upper, state, second)
        got = lax.ppermute(other.astype(BF16), AXES, [(i, i ^ step) for i in range(count)]).astype(F32)
        state = jnp.where(upper, jnp.concatenate([got, mine], axis=0), jnp.concatenate([mine, got], axis=0))
    return state, middle


def places(mesh):
    at = {(*d.coords, d.core_on_chip): i for i, d in enumerate(mesh.devices.flat)}
    return at, tuple(max(c[k] for c in at) + 1 for k in range(4))


def moves_to(layout, target):
    at, _ = layout
    return [(i, at[target(spot)]) for spot, i in at.items()]


def moves(layout, x=0, y=0, z=0, core=0):
    at, size = layout
    shift = (x, y, z, core)
    return [(i, at[tuple((c + s) % n for c, s, n in zip(spot, shift, size))]) for spot, i in at.items()]


def flip(layout, **by):
    masks = {i ^ j for i, j in moves(layout, **by)}
    return masks.pop() if len(masks) == 1 else None


def expert_kernel(*refs, width, capacity, local_count):
    shards, (chosen_ref, *weights), outs = refs[:8], refs[8:15], refs[15:23]
    block_ref, gate_w, up_w, down_w, sel_ref, pick_ref, gate_ref, back_ref, out_ref, in_sem, w_sem, out_sem = refs[23:]
    steps = 2 * local_count
    rows = shards[0].shape[0]
    pair_rows, slots = 2 * rows, 2 * capacity
    tile = width // 4
    packet = shards[0].shape[1]

    loads = [pltpu.make_async_copy(r, block_ref.at[i], in_sem.at[i]) for i, r in enumerate(shards)]
    fills = []
    for e in range(steps):
        part = weights[:3] if e < local_count else weights[3:]
        fills.append(
            [
                pltpu.make_async_copy(r.at[e % local_count], w.at[e % 2], w_sem.at[e, k])
                for k, (r, w) in enumerate(zip(part, (gate_w, up_w, down_w)))
            ]
        )
    for copy in loads + fills[0] + fills[1]:
        copy.start()

    before = lax.broadcasted_iota(jnp.int32, (pair_rows, pair_rows), 0)
    after = lax.broadcasted_iota(jnp.int32, (pair_rows, pair_rows), 1)
    earlier = jnp.where((before < after) & (before // rows == after // rows), 1.0, 0.0).astype(BF16)
    second = lax.broadcasted_iota(jnp.int32, (1, pair_rows), 1) // rows
    slot = lax.broadcasted_iota(jnp.int32, (slots, pair_rows), 0)
    for p in range(4):
        loads[2 * p].wait()
        loads[2 * p + 1].wait()
        marks = block_ref[2 * p : 2 * p + 2, :, width:].reshape(pair_rows, packet - width)
        gates = dot(chosen_ref[...], marks, ((1,), (1,)))
        named = jnp.where(gates != 0.0, 1.0, 0.0)
        rank = dot(named.astype(BF16), earlier).astype(jnp.int32)
        spot = jnp.where(gates != 0.0, rank + second * capacity, -1)
        for e in range(steps):
            hit = slot == spot[e : e + 1]
            pick_ref[p, e * slots : (e + 1) * slots, :] = jnp.where(hit, 1.0, 0.0).astype(BF16)
            gate = jnp.sum(jnp.where(hit, gates[e : e + 1], 0.0), axis=1, keepdims=True)
            gate_ref[e, p * slots : (p + 1) * slots, :] = jnp.broadcast_to(gate, (slots, 128))
        for n in range(4):
            cut = slice(n * tile, (n + 1) * tile)
            taken = dot(pick_ref[p], block_ref[2 * p : 2 * p + 2, :, cut].reshape(pair_rows, tile)).astype(BF16)
            for e in range(steps):
                sel_ref[e, p * slots : (p + 1) * slots, cut] = taken[e * slots : (e + 1) * slots]

    for e in range(steps):
        for copy in fills[e]:
            copy.wait()
        rows_in = sel_ref[e]
        gate, up = dot(rows_in, gate_w[e % 2]), dot(rows_in, up_w[e % 2])
        hidden = (gate / (1.0 + jnp.exp(-gate)) * up).astype(BF16)
        weight = gate_ref[e][:, 0:1]
        for n in range(4):
            cut = slice(n * tile, (n + 1) * tile)
            result = (dot(hidden, down_w[e % 2, :, cut]) * weight).astype(BF16)
            for p in range(4):
                back_ref[p, e * slots : (e + 1) * slots, cut] = result[p * slots : (p + 1) * slots]
        if e + 2 < steps:
            for copy in fills[e + 2]:
                copy.start()

    stores = [pltpu.make_async_copy(out_ref.at[i], r, out_sem.at[i]) for i, r in enumerate(outs)]
    for p in range(4):
        spread = pick_ref[p].astype(F32).T.astype(BF16)
        for n in range(4):
            cut = slice(n * tile, (n + 1) * tile)
            total = dot(spread, back_ref[p, :, cut]).astype(BF16)
            out_ref[2 * p : 2 * p + 2, :, cut] = total.reshape(2, rows, tile)
        stores[2 * p].start()
        stores[2 * p + 1].start()
    for copy in stores:
        copy.wait()


def run_experts(shards, chosen, mine, other, width, capacity):
    local_count, _, hidden = mine[0].shape
    steps = 2 * local_count
    slots = 2 * capacity
    rows, packet = shards[0].shape
    anywhere = pl.BlockSpec(memory_space=pl.ANY)
    return pl.pallas_call(
        functools.partial(expert_kernel, width=width, capacity=capacity, local_count=local_count),
        in_specs=[anywhere] * 8 + [pl.BlockSpec(memory_space=pltpu.VMEM)] + [anywhere] * 6,
        out_specs=[anywhere] * 8,
        out_shape=[jax.ShapeDtypeStruct((rows, width), BF16)] * 8,
        scratch_shapes=[
            pltpu.VMEM((8, rows, packet), BF16),
            pltpu.VMEM((2, width, hidden), BF16),
            pltpu.VMEM((2, width, hidden), BF16),
            pltpu.VMEM((2, hidden, width), BF16),
            pltpu.VMEM((steps, 4 * slots, width), BF16),
            pltpu.VMEM((4, steps * slots, 2 * rows), BF16),
            pltpu.VMEM((steps, 4 * slots, 128), F32),
            pltpu.VMEM((4, steps * slots, width), BF16),
            pltpu.VMEM((8, rows, width), BF16),
            pltpu.SemaphoreType.DMA((8,)),
            pltpu.SemaphoreType.DMA((steps, 3)),
            pltpu.SemaphoreType.DMA((8,)),
        ],
        cost_estimate=pl.CostEstimate(flops=width * hidden, bytes_accessed=rows * width, transcendentals=0),
        compiler_params=pltpu.CompilerParams(vmem_limit_bytes=32 * 2**20),
        name="experts",
    )(*shards, chosen, *mine, *other)


def plus(*parts):
    return sum(p.astype(F32) for p in parts[1:]) + parts[0].astype(F32)


def project_kernel(spots_ref, normed_ref, residual_ref, gain_ref, *refs, counts):
    parts, (mix_ref, routed_ref, sum_ref) = refs[:-3], refs[-3:]
    depth = normed_ref.shape[1]
    half = depth // 2
    low, high = normed_ref[:, :half], normed_ref[:, half:]
    odd = spots_ref[len(counts)] == 1
    mine, others = jnp.where(odd, high, low), jnp.where(odd, low, high)
    ordered = jnp.concatenate([mine, others], axis=1)
    first = 0
    for k, n in enumerate(counts):
        left = normed_ref[...] if n == 1 else ordered
        total, at = None, 0
        for w_ref in parts[first : first + n]:
            rows = w_ref.shape[0]
            product = dot(left[:, at : at + rows], w_ref[...])
            total = product if total is None else total + product
            at += rows
        first += n
        width = total.shape[1]
        sum_ref[:, pl.ds(pl.multiple_of(spots_ref[k] * width, width), width)] = total
    mix = (residual_ref[...].astype(F32) + sum_ref[...]).astype(BF16)
    mix_ref[...] = mix
    wide = mix.astype(F32)
    scale = lax.rsqrt(jnp.mean(wide * wide, axis=-1, keepdims=True) + EPS)
    routed_ref[...] = (wide * scale * gain_ref[...]).astype(BF16)


def project(spots, normed, residual, gain, parts):
    vmem = pl.BlockSpec(memory_space=pltpu.VMEM)
    flat = sum(parts, [])
    return pl.pallas_call(
        functools.partial(project_kernel, counts=[len(p) for p in parts]),
        in_specs=[pl.BlockSpec(memory_space=pltpu.SMEM)] + [vmem] * (3 + len(flat)),
        out_specs=[vmem] * 2,
        out_shape=[jax.ShapeDtypeStruct(residual.shape, BF16)] * 2,
        scratch_shapes=[pltpu.VMEM(residual.shape, F32)],
        cost_estimate=pl.CostEstimate(flops=1, bytes_accessed=residual.size, transcendentals=0),
        compiler_params=pltpu.CompilerParams(vmem_limit_bytes=24 * 2**20),
        name="project",
    )(spots, normed, residual, gain[None], *flat)


class Links:
    def __init__(self, layout):
        self.layout, self.sent = layout, {}

    def send(self, value, link, turn=1):
        queue = self.sent.setdefault(link, [])
        if len(queue) >= 2:
            value = tie(value, queue[-2])
        queue.append(lax.ppermute(value, AXES, moves(self.layout, **{link: turn})))
        return queue[-1]


def routed_by_gather(layout, place, twin, routed_in, gates, weights, other, capacity):
    rows, width = routed_in.shape
    experts = gates.shape[1]
    local_count = weights[0].shape[0]
    deep = layout[1][2]
    ids = jnp.concatenate([p * local_count + jnp.arange(local_count, dtype=jnp.int32) for p in (place, place ^ twin)])
    ids = jnp.pad(ids, (0, -ids.shape[0] % 8), constant_values=experts)
    chosen = (ids[:, None] == jnp.arange(experts, dtype=jnp.int32)).astype(BF16)
    pad = -(2 * experts) % 128
    chosen = jnp.pad(jnp.concatenate([chosen, chosen], axis=1), ((0, 0), (0, pad)))
    gates_hi, gates_lo = halves(gates)
    packet = jnp.concatenate([routed_in, gates_hi, gates_lo, jnp.zeros((rows, pad), BF16)], axis=1)
    packet = tie(packet, *other)

    links = Links(layout)
    here = {0: packet}
    by_x, by_y, far, sums = {}, {}, {}, {}
    pairs = [(t, t + 1) for t in range(0, deep, 2)]

    def spread(t):
        by_x[t], by_y[t] = links.send(here[t], "x"), links.send(here[t], "y")
        if t + 1 < deep:
            here[t + 1] = links.send(here[t], "z", -1)

    for a, b in pairs:
        if a == 0:
            spread(a)
            spread(b)
        far[a], far[b] = links.send(tie(by_x[a], by_y[b]), "y"), links.send(tie(by_y[b], by_x[b]), "x")
        ahead = [sums[a - 1][0]] if a else []
        if b + 1 < deep:
            spread(b + 1)
            spread(b + 2)
            ahead += [by_x[b + 2], by_y[b + 2]]
        shards = [d[t] for d in (here, by_x, by_y, far) for t in (a, b)]
        done = run_experts([tie(shards[0], *ahead), *shards[1:]], chosen, weights, other, width, capacity)
        sums[a], sums[b] = done[0::2], done[1::2]
    links = Links(layout)

    def own_turn(t, straight, with_far):
        part = plus(sums[t][0], straight, with_far)
        return lax.ppermute(part.astype(BF16), AXES, moves(layout, z=t)) if t else part

    def added(block, back):
        return plus(block, back).astype(BF16)

    back1 = links.send(sums[1][3], "x")
    back0 = links.send(tie(sums[0][3], back1), "y")
    straight1 = links.send(tie(sums[1][1], back1), "x")
    last1 = links.send(added(sums[1][2], back1), "y")
    total = [own_turn(1, straight1, last1)]
    for a, b in pairs[1:]:
        back_b, back_a = links.send(sums[b][3], "x"), links.send(sums[a][3], "y")
        last_a, straight_a = links.send(added(sums[a][1], back_a), "x"), links.send(sums[a][2], "y")
        total.append(own_turn(a, straight_a, last_a))
        straight_b, last_b = links.send(sums[b][1], "x"), links.send(added(sums[b][2], back_b), "y")
        total.append(own_turn(b, straight_b, last_b))
    last0 = links.send(added(tie(sums[0][1], total[0]), back0), "x")
    straight0 = links.send(tie(sums[0][2], total[0], back0), "y")
    return plus(own_turn(0, straight0, last0), *total)


def routed_by_exchange(routed_in, gates, named, weights, capacity):
    rows, width = routed_in.shape
    expert_gate, expert_up, expert_down = weights
    local_count, experts = expert_gate.shape[0], gates.shape[1]
    count = experts // local_count
    earlier = jnp.dot(jnp.tril(jnp.ones((rows, rows), BF16), -1), named.astype(BF16), preferred_element_type=F32)
    slot = jnp.where(named, earlier.astype(jnp.int32), capacity)
    picks = (slot.T[:, None, :] == jnp.arange(capacity, dtype=jnp.int32)[None, :, None]).reshape(experts * capacity, rows)
    outgoing = jnp.dot(picks.astype(BF16), routed_in, preferred_element_type=F32).astype(BF16)
    received = lax.all_to_all(
        outgoing.reshape(count, local_count, capacity, width), AXES, split_axis=0, concat_axis=0, tiled=True
    )
    received = received.transpose(1, 0, 2, 3).reshape(local_count, count * capacity, width)
    gate_part = jnp.einsum("esd,edf->esf", received, expert_gate, preferred_element_type=F32)
    up_part = jnp.einsum("esd,edf->esf", received, expert_up, preferred_element_type=F32)
    hidden = (jax.nn.silu(gate_part) * up_part).astype(BF16)
    result = jnp.einsum("esf,efd->esd", hidden, expert_down, preferred_element_type=F32).astype(BF16)
    result = result.reshape(local_count, count, capacity, width).transpose(1, 0, 2, 3)
    returned = lax.all_to_all(result, AXES, split_axis=0, concat_axis=0, tiled=True)
    spread = jnp.where(slot[:, :, None] == jnp.arange(capacity, dtype=jnp.int32), gates[:, :, None], 0.0)
    spread_hi, spread_lo = halves(spread.reshape(rows, experts * capacity))
    pulled = jnp.dot(
        jnp.concatenate([spread_hi, spread_lo], axis=0),
        returned.reshape(experts * capacity, width),
        preferred_element_type=F32,
    )
    return pulled[:rows] + pulled[rows:]


def local(
    layout,
    residual,
    mixed_qkv,
    output_gate,
    log_decay,
    write_strength,
    conv_weight,
    norm_gain,
    out_weight,
    post_gain,
    router_weight,
    expert_ids,
    expert_gate,
    expert_up,
    expert_down,
    shared_gate,
    shared_up,
    shared_down,
    shared_switch,
):
    rows, width = residual.shape
    head = norm_gain.shape[0]
    count = lax.axis_size(AXES)
    place = lax.axis_index(AXES)
    before = lax.ppermute(mixed_qkv[rows - 8 :], AXES, [(i, i + 1) for i in range(count - 1)])
    weights = (expert_gate, expert_up, expert_down)
    x, y, z, cores = layout[1]
    twin, facing = flip(layout, core=1), flip(layout, y=1)
    paired = (x, y, cores) == (2, 2, 2) and z % 2 == 0 and twin is not None
    columns = lax.axis_size("exp")
    beside = {i ^ j for i, j in moves_to(layout, lambda c: (c[0], c[1], c[2] ^ 1, c[3]))} if z % 2 == 0 else set()
    along = flip(layout, x=1)
    near = columns == 4 and None not in (twin, facing, along) and twin | facing == columns - 1 and len(beside) == 1
    swaps = [lax.ppermute(w, AXES, moves(layout, core=1)) for w in (weights if paired else ())]
    if near:
        swaps.append(lax.ppermute(out_weight, AXES, moves(layout, core=1)))
    block_map, read = delta_terms(mixed_qkv, before, conv_weight, log_decay, write_strength, head)
    half = out_weight.shape[0] // 2
    quarter = half // 2
    odd = ((place & min(beside)) != 0) ^ ((place & along) != 0) if near else None

    some = None
    if near:
        some = jnp.where(odd, out_weight[half:], out_weight[:half])
        some = [
            lax.ppermute(w, AXES, moves(layout, y=1))
            for w in lax.optimization_barrier((some[:quarter], some[quarter:], before))[:2]
        ]
    state, middle = starting_states(block_map, count, place, some, swaps)
    if near:
        pieces = tie(some[0], middle), tie(some[1], middle)
        rest = [
            lax.ppermute(pieces[0], AXES, moves(layout, x=1)),
            lax.ppermute(pieces[1], AXES, moves_to(layout, lambda c: (c[0], c[1], c[2] ^ 1, c[3]))),
        ]
        out_parts = [[out_weight], [*some, *rest], swaps[-1:]]
        out_parts.append([lax.ppermute(w, AXES, moves(layout, core=1)) for w in out_parts[1]])
        owners = [(place ^ mask) % columns for mask in (0, facing, twin, facing | twin)]
    normed = emit(read, state, output_gate, norm_gain)
    if near:
        spots = jnp.stack([jnp.int32(o) for o in owners] + [odd.astype(jnp.int32)])
        after_mix, routed_in = project(spots, normed, residual, post_gain, out_parts)
    else:
        projected = jnp.dot(normed, lax.all_gather(out_weight, "exp", axis=1, tiled=True), preferred_element_type=F32)
        after_mix = (residual.astype(F32) + projected).astype(BF16)
        after_wide = after_mix.astype(F32)
        scale = lax.rsqrt(jnp.mean(after_wide * after_wide, axis=-1, keepdims=True) + EPS)
        routed_in = (after_wide * scale * post_gain).astype(BF16)
    after_wide = after_mix.astype(F32)

    experts = expert_gate.shape[0] * count
    capacity = rows * expert_ids.shape[1] * 6 // (experts * 5)
    named = jnp.any(expert_ids[:, :, None] == jnp.arange(experts, dtype=jnp.int32), axis=1)
    logits = jnp.dot(routed_in, router_weight, preferred_element_type=F32)
    chosen = jnp.where(named, jnp.exp(jnp.where(named, logits, 0.0)), 0.0)
    gates = chosen / jnp.sum(chosen, axis=1, keepdims=True)
    if paired:
        routed = routed_by_gather(layout, place, twin, routed_in, gates, weights, swaps[:3], capacity)
    else:
        routed = routed_by_exchange(routed_in, gates, named, weights, capacity)
    shared_hidden = (
        jax.nn.silu(jnp.dot(routed_in, shared_gate, preferred_element_type=F32))
        * jnp.dot(routed_in, shared_up, preferred_element_type=F32)
    ).astype(BF16)
    switch = jax.nn.sigmoid(jnp.dot(routed_in, shared_switch, preferred_element_type=F32))
    shared_out = switch[:, None] * jnp.dot(shared_hidden, shared_down, preferred_element_type=F32)
    return (after_wide + routed + shared_out).astype(BF16)


def solution(mesh):
    rows = P(AXES, None)
    return jax.shard_map(
        functools.partial(local, places(mesh)),
        mesh=mesh,
        in_specs=(rows, rows, rows, rows, rows, P(), P(), P(None, "exp"), P(), P(), rows)
        + (P(AXES, None, None),) * 3
        + (P(),) * 4,
        out_specs=rows,
        check_vma=False,
    )
```
